128 devices in a mesh: gx: 8 (over y, core), gy: 16 (over z, x).
Axes of the slice: x: 4, y: 4, z: 4, core: 2. Of those that a mesh axis runs over, the one named last changes fastest.
Arguments:
- fluid_temp: float32 [256, 512, 512], P('gx', 'gy'), may hold values from -6 to 6
- kappa: bfloat16 [256, 512, 512], P('gx', 'gy'), may hold values from 0.019897461 to 0.13964844
- velocity: bfloat16 [3, 256, 512, 512], P(None, 'gx', 'gy'), may hold values from -0.19921875 to 0.19921875
- wall_temp: float32 [256, 512], P('gx', 'gy'), may hold values from -6 to 6
- face_count: int32 [128], P(('gx', 'gy')), may hold values from 1 to 8, 256 in all
- face_map: int32 [256], replicated, may hold values from 0 to 255, each once
- solid_temp: float32 [256, 32, 128], P(('gx', 'gy')), may hold values from -6 to 6
- solid_cond: float32 [256, 32, 128], P(('gx', 'gy')), may hold values from 0.5 to 2
- coolant: float32 [256, 128], P(('gx', 'gy')), may hold values from -6 to 6
Outputs:
- fluid_out: float32 [256, 512, 512], P('gx', 'gy')
- wall_out: float32 [256, 512], P('gx', 'gy')
- solid_out: float32 [256, 32, 128], P(('gx', 'gy'))
The draws below stay inside these ranges and needn't reach their ends.
Inputs may be any that keep to these rules, and one draw needn't show every extreme that they name: Each fluid device's first face_count face blocks are active; the counts add up to 256 and one device has exactly 8. `face_map`: A permutation: every solid face block is coupled to exactly one active fluid face block.
All inputs are finite; a program needn't handle non-finite values.
Results may differ from the reference program's by a relative error of at most 0.0014.
Values may be sent and summed in bfloat16 or wider, within the bound.
A program may use at most 128 MiB of HBM per device.

```python
import math
import jax
import jax.numpy as jnp
import numpy as np
from jax import lax

CX = 32
CY = 32
CZ = 512
FACE = 128
SZ = 32
SWEEPS = 6
FBD = 8
SBT = 256
NX = 256
NY = 512
N_GX = 8
N_GY = 16


def shard_levels(key, dims, pieces, low, largest):
    loudness, own = 1.0, jax.random.fold_in(key, 6)
    for position, parts in pieces:
        draws = jnp.exp(jax.random.uniform(jax.random.fold_in(own, position), (parts,), jnp.float32, low / len(pieces), largest / len(pieces)))
        loudness = loudness * jnp.repeat(draws, dims[position] // parts).reshape([-1 if axis == position else 1 for axis in range(len(dims))])
    return loudness


def length_profile(count, total, limit, slope):
    weights = [(1 << 20) // math.isqrt(rank ** slope) + 1 for rank in range(2, count + 1)]
    spare, counts = total - limit - (count - 1), [1] * (count - 1)
    while spare > 0:
        free = [i for i in range(count - 1) if counts[i] < limit]
        pool, budget = sum([weights[i] for i in free]), spare
        for i in free:
            addition = min(limit - counts[i], max(1, budget * weights[i] // pool), spare)
            counts[i] = counts[i] + addition
            spare = spare - addition
    return np.array([limit] + counts)


def uneven_parts(key, count, total, limit, skew):
    if count == 2:
        one = jax.random.randint(key, (), max(1, total - limit), min(limit, total - 1) + 1)
        return jnp.stack([one, total - one])
    sizes = jnp.asarray(length_profile(count, total, limit, skew), jnp.int32)
    couples = (count - 1) // 2
    source_of, taker = sizes[1:1 + 2 * couples:2], sizes[2:2 + 2 * couples:2]
    margin = jnp.minimum(source_of - 1, limit - taker)
    passed = jax.random.randint(jax.random.fold_in(key, 1), (couples,), 0, 1 << 20) % (margin + 1)
    sizes = sizes.at[1:1 + 2 * couples:2].set(source_of - passed).at[2:2 + 2 * couples:2].set(taker + passed)
    return sizes[jax.random.permutation(jax.random.fold_in(key, 2), count)]


def noise(stream_key, dims, deviation, limit, cuts=(), held_as=jnp.bfloat16):
    factor_of = shard_levels(stream_key, dims, cuts, -0.22, 0.18) if cuts else 1.0
    array = jax.random.normal(stream_key, dims, jnp.float32) * deviation * factor_of
    return jnp.minimum(jnp.maximum(array, -limit), limit).astype(held_as)


def setup_inputs(seed: int = 0) -> dict:
    keys = jax.random.split(jax.random.key(seed), 10)
    return {
        "fluid_temp": noise(keys[0], (NX, NY, CZ), 1.0, 6.0, ((0, 8), (1, 16)), jnp.float32),
        "kappa": jnp.clip(jnp.exp(math.log(0.13964844) - 1.94853597 * jax.random.uniform(keys[1], (NX, NY, CZ), jnp.float32) ** shard_levels(keys[1], (NX, NY, CZ), ((0, 8), (1, 16)), -0.2, 0.2)), 0.019897461, 0.13964844).astype(jnp.bfloat16),
        "velocity": noise(keys[2], (3, NX, NY, CZ), 0.05, 0.19921875, ((1, 8), (2, 16))),
        "wall_temp": noise(keys[3], (NX, NY), 1.0, 6.0, ((0, 8), (1, 16)), jnp.float32),
        "face_count": uneven_parts(keys[4], N_GX * N_GY, SBT, FBD, 2).astype(jnp.int32),
        "face_map": jax.random.permutation(keys[5], SBT).astype(jnp.int32),
        "solid_temp": noise(keys[6], (SBT, SZ, FACE), 1.0, 6.0, ((0, 128),), jnp.float32),
        "solid_cond": jnp.clip(jnp.exp(math.log(2.0) - 1.3862944 * jax.random.uniform(keys[7], (SBT, SZ, FACE), jnp.float32) ** shard_levels(keys[7], (SBT, SZ, FACE), ((0, 128),), -0.2, 0.2)), 0.5, 2.0),
        "coolant": noise(keys[8], (SBT, FACE), 1.0, 6.0, ((0, 128),), jnp.float32),
    }


wall_ratio = 25.0
cool_coef = 1.0


def face_term(center, cond_mid, neighbor, cond_nb, flow_nb, flow_mid, orient):
    face_cond = 0.5 * (cond_mid + cond_nb)
    face_flow = 0.5 * (flow_mid + flow_nb)
    return face_cond * (neighbor - center) - orient * face_flow * 0.5 * (center + neighbor)


def advance(padded, wall_plane, cond_pad, flow_x, flow_y, flow_z):
    center = padded[1:-1, 1:-1]
    cond_mid = cond_pad[1:-1, 1:-1].astype(jnp.float32)
    mid_x = flow_x[1:-1, 1:-1].astype(jnp.float32)
    mid_y = flow_y[1:-1, 1:-1].astype(jnp.float32)
    mid_z = flow_z.astype(jnp.float32)
    updated = center + face_term(center, cond_mid, padded[2:, 1:-1], cond_pad[2:, 1:-1].astype(jnp.float32), flow_x[2:, 1:-1].astype(jnp.float32), mid_x, 1.0)
    updated = updated + face_term(center, cond_mid, padded[:-2, 1:-1], cond_pad[:-2, 1:-1].astype(jnp.float32), flow_x[:-2, 1:-1].astype(jnp.float32), mid_x, -1.0)
    updated = updated + face_term(center, cond_mid, padded[1:-1, 2:], cond_pad[1:-1, 2:].astype(jnp.float32), flow_y[1:-1, 2:].astype(jnp.float32), mid_y, 1.0)
    updated = updated + face_term(center, cond_mid, padded[1:-1, :-2], cond_pad[1:-1, :-2].astype(jnp.float32), flow_y[1:-1, :-2].astype(jnp.float32), mid_y, -1.0)
    zero_col = jnp.zeros_like(center[..., :1])
    upper = jnp.concatenate([center[..., 1:], zero_col], axis=-1)
    lower = jnp.concatenate([wall_plane[..., None], center[..., :-1]], axis=-1)
    cond_up = jnp.concatenate([cond_mid[..., 1:], zero_col], axis=-1)
    cond_down = jnp.concatenate([zero_col, cond_mid[..., :-1]], axis=-1)
    flow_up = jnp.concatenate([mid_z[..., 1:], zero_col], axis=-1)
    flow_down = jnp.concatenate([zero_col, mid_z[..., :-1]], axis=-1)
    updated = updated + face_term(center, cond_mid, upper, cond_up, flow_up, mid_z, 1.0)
    updated = updated + face_term(center, cond_mid, lower, cond_down, flow_down, mid_z, -1.0)
    return updated


def sweeps(temps, conds, near_wall, wall_cond, coolant):
    nblk, layers, width = temps.shape
    heat_wall = wall_ratio * wall_cond
    depth_cond = 0.5 * (conds[:, 1:] + conds[:, :-1])
    side_cond = 0.5 * (conds[:, :, 1:] + conds[:, :, :-1])
    zero_layer = jnp.zeros((nblk, 1, width), jnp.float32)
    zero_side = jnp.zeros((nblk, layers, 1), jnp.float32)
    middle = jnp.zeros((nblk, layers - 2, width), jnp.float32)
    cond_up = jnp.concatenate([zero_layer, depth_cond], axis=1)
    cond_down = jnp.concatenate([depth_cond, zero_layer], axis=1)
    cond_left = jnp.concatenate([zero_side, side_cond], axis=2)
    cond_right = jnp.concatenate([side_cond, zero_side], axis=2)
    bound_coef = jnp.concatenate([heat_wall[:, None, :], middle, jnp.full((nblk, 1, width), cool_coef, jnp.float32)], axis=1)
    source = jnp.concatenate([(heat_wall * near_wall)[:, None, :], middle, (cool_coef * coolant)[:, None, :]], axis=1)
    denom = cond_up + cond_down + cond_left + cond_right + bound_coef
    for repeat in range(SWEEPS):
        neighbors = cond_up * jnp.concatenate([zero_layer, temps[:, :-1]], axis=1)
        neighbors = neighbors + cond_down * jnp.concatenate([temps[:, 1:], zero_layer], axis=1)
        neighbors = neighbors + cond_left * jnp.concatenate([zero_side, temps[:, :, :-1]], axis=2)
        neighbors = neighbors + cond_right * jnp.concatenate([temps[:, :, 1:], zero_side], axis=2)
        temps = (neighbors + source) / denom
    return temps


def to_blocks(plane):
    return plane.reshape(N_GX, CX, N_GY, CY).transpose(0, 2, 1, 3).reshape(N_GX * N_GY * FBD, FACE)


def from_blocks(blocks):
    return blocks.reshape(N_GX, N_GY, CX, CY).transpose(0, 2, 1, 3).reshape(NX, NY)


def reference(fluid_temp, kappa, velocity, wall_temp, face_count, face_map, solid_temp, solid_cond, coolant):
    temp_pad = jnp.pad(fluid_temp, ((2, 2), (1, 1), (0, 0)))
    cond_pad = jnp.pad(kappa, ((2, 2), (1, 1), (0, 0)))
    flow_pad = jnp.pad(velocity, ((0, 0), (2, 2), (1, 1), (0, 0)))
    wall_pad = jnp.pad(wall_temp, ((2, 2), (0, 0)))

    def slab(slab_index):
        start = slab_index * CX
        temp_s = lax.dynamic_slice_in_dim(temp_pad, start, CX + 4, 0)
        cond_s = lax.dynamic_slice_in_dim(cond_pad, start, CX + 4, 0)
        flow_s = lax.dynamic_slice_in_dim(flow_pad, start, CX + 4, 1)
        wall_s = lax.dynamic_slice_in_dim(wall_pad, start, CX + 4, 0)
        first = advance(temp_s, wall_s[1:-1], cond_s, flow_s[0], flow_s[1], flow_s[2][1:-1, 1:-1])
        row_ids = start - 1 + jnp.arange(CX + 2, dtype=jnp.int32)
        inside = (row_ids >= 0) & (row_ids < NX)
        first = jnp.where(inside[:, None, None], first, jnp.float32(0.0))
        first_pad = jnp.pad(first, ((0, 0), (1, 1), (0, 0)))
        return advance(first_pad, wall_s[2:-2], cond_s[1:-1], flow_s[0][1:-1], flow_s[1][1:-1], flow_s[2][2:-2, 1:-1])

    fluid_out = lax.map(slab, jnp.arange(N_GX, dtype=jnp.int32)).reshape(NX, NY, CZ)
    near_blocks = to_blocks(fluid_out[:, :, 0])
    cond_blocks = to_blocks(0.5 * kappa[:, :, 0].astype(jnp.float32))
    inclusive = jnp.cumsum(face_count).astype(jnp.int32)
    offsets = inclusive - face_count
    ranks = jnp.arange(SBT, dtype=jnp.int32)
    source_dev = jnp.sum((inclusive[None, :] <= ranks[:, None]).astype(jnp.int32), axis=1).astype(jnp.int32)
    fluid_slot = source_dev * FBD + ranks - offsets[source_dev]
    near_wall = jnp.zeros((SBT, FACE), jnp.float32).at[face_map].set(near_blocks[fluid_slot])
    wall_cond = jnp.zeros((SBT, FACE), jnp.float32).at[face_map].set(cond_blocks[fluid_slot])
    solid_out = sweeps(solid_temp, solid_cond, near_wall, wall_cond, coolant)
    wall_blocks = to_blocks(wall_temp).at[fluid_slot].set(solid_out[face_map, 0, :])
    return fluid_out, from_blocks(wall_blocks), solid_out
```

```python
import functools

import jax
import jax.numpy as jnp
from jax import lax
from jax.experimental import pallas as pl
from jax.experimental.pallas import tpu as pltpu
from jax.sharding import PartitionSpec as P

MESH = pl.DeviceIdType.MESH
F32 = jnp.float32
SWEEPS = 6
WALL_RATIO = 25.0
COOL = 1.0
EXACT = lax.Precision.HIGHEST
PAD = 8


def nt_dot(a, b, precision=None):
    return lax.dot_general(
        a, b, (((1,), (1,)), ((), ())), precision=precision, preferred_element_type=F32
    )


def iota(shape, axis):
    return lax.broadcasted_iota(jnp.int32, shape, axis)


def slab_step(temp, k0, ux, uy, uz, wall, t_nb, k_nb, u_nb):
    rows = temp.shape[0]
    row = iota(temp.shape, 0)
    out = temp
    for pos, (sign, own) in enumerate(((1, ux), (-1, ux), (1, uy), (-1, uy))):
        kk, uu, n = k0 + k_nb[pos], own + u_nb[pos], t_nb[pos]
        out = out + kk * (n - temp) - sign * uu * (temp + n)
    up = pltpu.roll(temp, rows - 1, 0)
    kk, uu = k0 + pltpu.roll(k0, rows - 1, 0), uz + pltpu.roll(uz, rows - 1, 0)
    out = out + kk * (up - temp) - uu * (temp + up)
    first = row == 0
    down = jnp.where(first, wall, pltpu.roll(temp, 1, 0))
    kk = k0 + jnp.where(first, 0.0, pltpu.roll(k0, 1, 0))
    uu = uz + jnp.where(first, 0.0, pltpu.roll(uz, 1, 0))
    return out + kk * (down - temp) + uu * (temp + down)


def kernel(
    ngx, ngy,
    t_hbm, k_hbm, v_hbm, wall_ref, count_ref, map_ref, st_ref, sc_ref, cool_ref,
    fluid_ref, wallout_ref, solid_ref,
    tp, t1p, kp, uxp, uyp, uzp, coef, kraw, vraw, wallb,
    ys_send, ys_recv, y1_send, y1_recv,
    wy_send, wy_recv, wx_send, wx_recv, vy_send, vy_recv, vx_send, vx_recv,
    cbuf, csend, cc, nb, m3s, m3r, surf,
    ld_sem, hs, hr, t1s, t1r, ws, wr, v2s, v2r, gs, gr, out_sem, rel,
):
    nx, ny, nz = t_hbm.shape
    cells = nx * ny
    nblk = cells // 128
    ndev = ngx * ngy
    nsolid = 2 * ndev
    i, j = lax.axis_index("gx"), lax.axis_index("gy")
    me = i * ngy + j

    def gxd(k):
        return (lax.rem(i + k + ngx, ngx), j)

    def gyd(k):
        return (i, lax.rem(j + k + ngy, ngy))

    def hello(sem, targets):
        for target in targets:
            pl.semaphore_signal(sem, inc=1, device_id=target, device_id_type=MESH)

    barrier = pltpu.get_barrier_semaphore()
    near4 = [gxd(1), gxd(-1), gyd(1), gyd(-1)]
    hello(barrier, near4)
    inside = (pl.ds(1, nx), pl.ds(PAD, ny), slice(None))
    load_k = pltpu.make_async_copy(k_hbm, kraw, ld_sem.at[0])
    load_v = pltpu.make_async_copy(v_hbm, vraw, ld_sem.at[1])
    load_t = pltpu.make_async_copy(t_hbm, tp.at[inside], ld_sem.at[2])
    load_t.start()
    load_k.start()
    load_v.start()

    eye = iota((ny, ny), 0) == iota((ny, ny), 1)

    def wall_body(x, carry):
        line = wall_ref[pl.ds(x, 1), :]
        col = jnp.sum(jnp.where(eye, jnp.broadcast_to(line, (ny, ny)), 0.0), axis=1, keepdims=True)
        wallb[x] = jnp.broadcast_to(col, (ny, 128))
        return carry

    lax.fori_loop(0, nx, wall_body, 0)

    for cond, plane in ((i == 0, 0), (i == ngx - 1, nx + 1)):

        @pl.when(cond)
        def _():
            tp[plane] = jnp.zeros(tp.shape[1:], F32)
            t1p[plane] = jnp.zeros(t1p.shape[1:], F32)
            kp[plane] = jnp.zeros(kp.shape[1:], F32)
            uxp[plane] = jnp.zeros(uxp.shape[1:], F32)
            side = 0 if plane == 0 else 1
            wx_recv[side] = jnp.zeros(wx_recv.shape[1:], F32)
            vx_recv[side] = jnp.zeros(vx_recv.shape[1:], F32)

    for cond, side in ((j == 0, 0), (j == ngy - 1, 1)):

        @pl.when(cond)
        def _():
            ys_recv[side] = jnp.zeros(ys_recv.shape[1:], F32)
            y1_recv[side] = jnp.zeros(y1_recv.shape[1:], F32)
            wy_recv[side] = jnp.zeros(wy_recv.shape[1:], F32)
            vy_recv[side] = jnp.zeros(vy_recv.shape[1:], F32)

    pl.semaphore_wait(barrier, 4)
    hello(rel.at[0], near4)

    def halo(src_of, dst_of, send, recv, axis):
        def make(up):
            spot, size, dev = (i, ngx, gxd) if axis == 0 else (j, ngy, gyd)
            copy = pltpu.make_async_remote_copy(
                src_ref=src_of(up), dst_ref=dst_of(up),
                send_sem=send.at[up], recv_sem=recv.at[up],
                device_id=dev(1 if up else -1), device_id_type=MESH,
            )
            sends = spot < size - 1 if up else spot > 0
            gets = spot > 0 if up else spot < size - 1
            return copy, sends, gets

        pairs = [make(1), make(0)]

        def start():
            for copy, sends, gets in pairs:
                pl.when(sends)(copy.start)

        def wait_recv():
            for copy, sends, gets in pairs:
                pl.when(gets)(copy.wait_recv)

        def wait_send():
            for copy, sends, gets in pairs:
                pl.when(sends)(copy.wait_send)

        return start, wait_recv, wait_send

    wy = halo(lambda up: wy_send, lambda up: wy_recv.at[1 - up], ws.at[0], wr.at[0], 1)
    wx = halo(lambda up: wx_send.at[up], lambda up: wx_recv.at[1 - up], ws.at[1], wr.at[1], 0)
    vy = halo(lambda up: vy_send, lambda up: vy_recv.at[1 - up], v2s.at[0], v2r.at[0], 1)
    vx = halo(lambda up: vx_send.at[up], lambda up: vx_recv.at[1 - up], v2s.at[1], v2r.at[1], 0)
    ys = halo(lambda up: ys_send.at[up], lambda up: ys_recv.at[1 - up], hs.at[0], hr.at[0], 1)

    def planes(ref, padded):
        rows = pl.ds(PAD, ny) if padded else pl.ds(0, ny)
        return (
            lambda up: ref.at[nx if up else 1, rows],
            lambda up: ref.at[0 if up else nx + 1, rows],
        )

    xt = halo(*planes(tp, True), hs.at[1], hr.at[1], 0)
    xk = halo(*planes(kp, True), hs.at[2], hr.at[2], 0)
    xu = halo(*planes(uxp, False), hs.at[3], hr.at[3], 0)
    y1 = halo(lambda up: y1_send.at[up], lambda up: y1_recv.at[1 - up], t1s.at[0], t1r.at[0], 1)
    x1 = halo(*planes(t1p, True), t1s.at[1], t1r.at[1], 0)

    load_t.wait()
    load_k.wait()
    load_v.wait()
    xt[0]()

    pick = (iota((8, 128), 0) == iota((8, 128), 1)).astype(F32)
    pick16 = pick.astype(jnp.bfloat16)

    def slab(value, exact):
        value = value.reshape(cells, 128)
        return nt_dot(pick, value, EXACT) if exact else nt_dot(pick16, value)

    s_t = slab(tp[1 : nx + 1, PAD : PAD + ny, 0:128], True)
    s_w = slab(wallb[...], True)[0:1]
    s_k = 0.5 * slab(kraw[:, :, 0:128], False)
    s_ux = 0.25 * slab(vraw[0, :, :, 0:128], False)
    s_uy = 0.25 * slab(vraw[1, :, :, 0:128], False)
    s_uz = 0.25 * slab(vraw[2, :, :, 0:128], False)
    wy_send[0:2, :] = s_t[0:2]
    wy_send[2:4, :] = s_k[0:2]
    wy_send[4:6, :] = s_uy[0:2]
    wy_send[6:8, :] = jnp.zeros((2, cells), F32)
    for up, lanes in ((1, slice(cells - 128, cells)), (0, slice(0, 128))):
        wx_send[up, 0:2, :] = s_t[0:2, lanes]
        wx_send[up, 2:4, :] = s_k[0:2, lanes]
        wx_send[up, 4:6, :] = s_ux[0:2, lanes]
        wx_send[up, 6:8, :] = jnp.zeros((2, 128), F32)
    wy[0]()
    wx[0]()

    pl.semaphore_wait(rel.at[0], 4)
    hello(rel.at[1], [gxd(2), gxd(-2), gyd(2), gyd(-2)])

    def convert(x, carry):
        kv = 0.5 * kraw[x].astype(F32)
        kp[x + 1, PAD : PAD + ny, :] = kv
        uxp[x + 1] = 0.25 * vraw[0, x].astype(F32)
        uv = 0.25 * vraw[1, x].astype(F32)
        uyp[x, PAD : PAD + ny, :] = uv
        uzp[x] = 0.25 * vraw[2, x].astype(F32)
        ys_send[0, 0, x] = tp[x + 1, PAD : PAD + 1, :]
        ys_send[1, 0, x] = tp[x + 1, PAD + ny - 1 : PAD + ny, :]
        ys_send[0, 1, x] = kv[0:1]
        ys_send[1, 1, x] = kv[ny - 1 : ny]
        ys_send[0, 2, x] = uv[0:1]
        ys_send[1, 2, x] = uv[ny - 1 : ny]
        return carry

    lax.fori_loop(0, nx, convert, 0)
    ys[0]()
    xk[0]()
    xu[0]()

    pl.semaphore_wait(rel.at[1], 4)
    hello(rel.at[2], [gyd(4), gyd(-4)])

    counts = jnp.full((8, 128), count_ref[0], jnp.int32).astype(F32)
    csend[...] = counts

    def spread(src, buf, slot, size, dev, sem, rsem):
        for k in range(1, size):
            pltpu.make_async_remote_copy(
                src_ref=src(k), dst_ref=buf.at[slot], send_sem=sem, recv_sem=rsem,
                device_id=dev(k), device_id_type=MESH,
            ).start()

    def all_in(buf, size, sem):
        part = buf.at[pl.ds(0, size - 1)]
        pltpu.make_async_copy(part, part, sem).wait()

    spread(lambda k: csend, cbuf, i, ngx, gxd, gs.at[0], gr.at[0])

    lane = iota((8, cells), 1)
    y_first, y_last = lax.rem(lane, ny) == 0, lax.rem(lane, ny) == ny - 1
    x_first, x_last = lane < ny, lane >= cells - ny

    def y_neighbours(own, low, high):
        plus = jnp.where(y_last, pltpu.roll(high, ny - 1, 1), pltpu.roll(own, cells - 1, 1))
        minus = jnp.where(y_first, pltpu.roll(low, cells - (ny - 1), 1), pltpu.roll(own, 1, 1))
        return plus, minus

    def widen(tile):
        return jnp.concatenate([tile] * (cells // 128), axis=1)

    def x_neighbours(own, low, high):
        plus = jnp.where(x_last, widen(pltpu.roll(high, 128 - ny, 1)), pltpu.roll(own, cells - ny, 1))
        minus = jnp.where(x_first, widen(pltpu.roll(low, ny, 1)), pltpu.roll(own, ny, 1))
        return plus, minus

    wy[1]()
    wx[1]()

    def rows_of(value, part):
        return pltpu.roll(value, 8 - 2 * part, 0) if part else value

    ylow, yhigh, xlow, xhigh = wy_recv[0], wy_recv[1], wx_recv[0], wx_recv[1]
    ty = y_neighbours(s_t, rows_of(ylow, 0), rows_of(yhigh, 0))
    ky = y_neighbours(s_k, rows_of(ylow, 1), rows_of(yhigh, 1))
    uy = y_neighbours(s_uy, rows_of(ylow, 2), rows_of(yhigh, 2))
    tx = x_neighbours(s_t, rows_of(xlow, 0), rows_of(xhigh, 0))
    kx = x_neighbours(s_k, rows_of(xlow, 1), rows_of(xhigh, 1))
    ux = x_neighbours(s_ux, rows_of(xlow, 2), rows_of(xhigh, 2))
    k_nb, u_nb = kx + ky, ux + uy
    first = slab_step(s_t, s_k, s_ux, s_uy, s_uz, s_w, tx + ty, k_nb, u_nb)
    vy_send[...] = first
    vx_send[1] = first[:, cells - 128 :]
    vx_send[0] = first[:, 0:128]
    vy[0]()
    vx[0]()

    cbuf[i] = counts
    cond_blocks = jnp.concatenate([s_k[0:1, 128 * b : 128 * b + 128] for b in range(nblk)], axis=0)
    all_in(cbuf, ngx, gr.at[0])
    row8 = iota((8, 128), 0)
    column = jnp.zeros((8, 128), F32)
    for k in range(ngx):
        column = column + jnp.where(row8 == k, cbuf[k], 0.0)
    cc[j, 0:8] = cond_blocks
    cc[j, 8:16] = column
    pl.semaphore_wait(rel.at[2], 2)
    spread(lambda k: cc.at[j], cc, j, ngy, gyd, gs.at[1], gr.at[1])

    vy[1]()
    vx[1]()
    ty = y_neighbours(first, vy_recv[0], vy_recv[1])
    tx = x_neighbours(first, vx_recv[0], vx_recv[1])
    second = slab_step(first, s_k, s_ux, s_uy, s_uz, s_w, tx + ty, k_nb, u_nb)
    nb[j] = jnp.concatenate([second[0:1, 128 * b : 128 * b + 128] for b in range(nblk)], axis=0)
    spread(lambda k: nb.at[j], nb, j, ngy, gyd, gs.at[2], gr.at[2])

    ys[1]()
    xk[1]()
    xu[1]()
    zlane = iota((8, nz), 1)
    z_first, z_last = zlane == 0, zlane == nz - 1

    def coef_body(x, carry):
        kp[x + 1, PAD - 1 : PAD, :] = ys_recv[0, 1, x]
        kp[x + 1, PAD + ny : PAD + ny + 1, :] = ys_recv[1, 1, x]
        uyp[x, PAD - 1 : PAD, :] = ys_recv[0, 2, x]
        uyp[x, PAD + ny : PAD + ny + 1, :] = ys_recv[1, 2, x]
        tp[x + 1, PAD - 1 : PAD, :] = ys_recv[0, 0, x]
        tp[x + 1, PAD + ny : PAD + ny + 1, :] = ys_recv[1, 0, x]
        for yt in range(0, ny, 8):
            y0 = PAD + yt
            k0 = kp[x + 1, y0 : y0 + 8, :]
            ux0 = uxp[x + 1, yt : yt + 8, :]
            uy0 = uyp[x, y0 : y0 + 8, :]
            uz0 = uzp[x, yt : yt + 8, :]
            here = pl.ds(yt, 8)
            kk, uu = k0 + kp[x + 2, y0 : y0 + 8, :], ux0 + uxp[x + 2, yt : yt + 8, :]
            coef[1, x, here] = kk - uu
            total = kk + uu
            kk, uu = k0 + kp[x, y0 : y0 + 8, :], ux0 + uxp[x, yt : yt + 8, :]
            coef[2, x, here] = kk + uu
            total = total + (kk - uu)
            kk, uu = k0 + kp[x + 1, y0 + 1 : y0 + 9, :], uy0 + uyp[x, y0 + 1 : y0 + 9, :]
            coef[3, x, here] = kk - uu
            total = total + (kk + uu)
            kk, uu = k0 + kp[x + 1, y0 - 1 : y0 + 7, :], uy0 + uyp[x, y0 - 1 : y0 + 7, :]
            coef[4, x, here] = kk + uu
            total = total + (kk - uu)
            kk = k0 + jnp.where(z_last, 0.0, pltpu.roll(k0, nz - 1, 1))
            uu = uz0 + jnp.where(z_last, 0.0, pltpu.roll(uz0, nz - 1, 1))
            coef[5, x, here] = jnp.where(z_last, 0.0, kk - uu)
            total = total + (kk + uu)
            kk = k0 + jnp.where(z_first, 0.0, pltpu.roll(k0, 1, 1))
            uu = uz0 + jnp.where(z_first, 0.0, pltpu.roll(uz0, 1, 1))
            coef[6, x, here] = kk + uu
            total = total + (kk - uu)
            coef[0, x, here] = 1.0 - total
        return carry

    lax.fori_loop(0, nx, coef_body, 0)

    def step_at(src, x, yt):
        y0 = PAD + yt
        here = pl.ds(yt, 8)
        mid = src[x + 1, y0 : y0 + 8, :]
        wall = jnp.concatenate([wallb[x, here]] * (nz // 128), axis=1)
        down = jnp.where(z_first, wall, pltpu.roll(mid, 1, 1))
        out = coef[0, x, here] * mid
        out = out + coef[1, x, here] * src[x + 2, y0 : y0 + 8, :]
        out = out + coef[2, x, here] * src[x, y0 : y0 + 8, :]
        out = out + coef[3, x, here] * src[x + 1, y0 + 1 : y0 + 9, :]
        out = out + coef[4, x, here] * src[x + 1, y0 - 1 : y0 + 7, :]
        out = out + coef[5, x, here] * pltpu.roll(mid, nz - 1, 1)
        return out + coef[6, x, here] * down

    xt[1]()

    def first_body(x, carry):
        for yt in range(0, ny, 8):
            value = step_at(tp, x, yt)
            t1p[x + 1, PAD + yt : PAD + yt + 8, :] = value
            if yt == 0:
                y1_send[0, x] = value[0:1]
            if yt == ny - 8:
                y1_send[1, x] = value[7:8]
        return carry

    lax.fori_loop(0, nx, first_body, 0)
    y1[0]()
    x1[0]()

    all_in(cc, ngy, gr.at[1])
    q = iota((8, 128), 1)
    table = jnp.zeros((8, 128), F32)
    for k in range(ngy):
        table = table + jnp.where(q // nblk == k, cc[k, 8:16], 0.0)
    before = (iota((128, 128), 0) // nblk < iota((128, 128), 1) // nblk).astype(F32) * (1.0 / nblk)
    prefix = jnp.dot(table, before, precision=EXACT, preferred_element_type=F32)
    row_total = jnp.sum(table, axis=1, keepdims=True) * (1.0 / nblk)
    offset = jnp.sum(
        jnp.where(row8 == i, prefix, 0.0) + jnp.where(row8 < i, jnp.broadcast_to(row_total, (8, 128)), 0.0),
        axis=0, keepdims=True,
    )
    mine = jnp.sum(jnp.where(row8 == i, table, 0.0), axis=0, keepdims=True)
    slot = lax.rem(iota((1, 128), 1), nblk).astype(F32)
    live = slot < mine
    rank = jnp.where(live, offset + slot, -1.0)
    onehot = (iota((nsolid, 128), 0).astype(F32) == rank).astype(F32)
    fmap = map_ref[...].astype(F32)
    target = jnp.dot(fmap, onehot, precision=EXACT, preferred_element_type=F32)
    target = jnp.where(live, target, -1.0)
    line = iota((8 * ngx, 128), 0)
    kind = lax.rem(line, 8)
    owner = 2 * ((line // 8) * ngy + j)
    for_near = jnp.where(kind < 2, owner + kind, -2).astype(F32)
    for_cond = jnp.where((kind >= 2) & (kind < 4), owner + kind - 2, -2).astype(F32)
    w_near = (for_near == target).astype(F32)
    w_cond = (for_cond == target).astype(F32)
    cond_rows = cc[:, 0:8].reshape(ngy * 8, 128)
    payload_c = jnp.dot(w_cond[:, : ngy * 8], cond_rows, precision=EXACT, preferred_element_type=F32)

    all_in(nb, ngy, gr.at[2])
    payload = payload_c + jnp.dot(
        w_near[:, : ngy * 8], nb[...].reshape(ngy * 8, 128), precision=EXACT, preferred_element_type=F32
    )
    m3s[...] = payload.reshape(ngx, 8, 128)
    spread(lambda k: m3s.at[gxd(k)[0]], m3r, i, ngx, gxd, gs.at[3], gr.at[3])
    m3r[i] = m3s[i]

    y1[1]()
    x1[1]()

    def second_body(x, carry):
        t1p[x + 1, PAD - 1 : PAD, :] = y1_recv[0, x]
        t1p[x + 1, PAD + ny : PAD + ny + 1, :] = y1_recv[1, x]
        for yt in range(0, ny, 8):
            fluid_ref[x, pl.ds(yt, 8)] = step_at(t1p, x, yt)
        return carry

    lax.fori_loop(0, nx, second_body, 0)

    own = iota((8, 128), 1) // nblk == j
    start = jnp.sum(jnp.where((row8 == 0) & own, jnp.broadcast_to(offset, (8, 128)), 0.0)) * (1.0 / nblk)
    slot8 = iota((8, nsolid), 0)
    rank8 = jnp.where(slot8 < count_ref[0], start + slot8.astype(F32), -1.0)
    onehot8 = (iota((8, nsolid), 1).astype(F32) == rank8).astype(F32)
    gline = iota((nsolid, nsolid), 0)
    gid = (2 * lax.rem(gline, ndev) + gline // ndev).astype(F32)
    holds = (gid == fmap).astype(F32)
    fetch = nt_dot(onehot8, holds)

    layers, width = st_ref.shape[1:]
    lines = 2 * layers
    conds = sc_ref[...].reshape(lines, width)
    temps = st_ref[...].reshape(lines, width)
    srow = lax.rem(iota((lines, width), 0), layers)
    scol = iota((lines, width), 1)
    c_up = jnp.where(srow == 0, 0.0, 0.5 * (conds + pltpu.roll(conds, 1, 0)))
    c_dn = jnp.where(srow == layers - 1, 0.0, 0.5 * (conds + pltpu.roll(conds, lines - 1, 0)))
    c_lf = jnp.where(scol == 0, 0.0, 0.5 * (conds + pltpu.roll(conds, 1, 1)))
    c_rt = jnp.where(scol == width - 1, 0.0, 0.5 * (conds + pltpu.roll(conds, width - 1, 1)))
    cool = cool_ref[...]

    def per_block(a, b):
        return jnp.concatenate(
            [jnp.broadcast_to(a, (layers, width)), jnp.broadcast_to(b, (layers, width))], axis=0
        )

    cool_at = per_block(cool[0:1], cool[1:2])

    all_in(m3r, ngx, gr.at[3])
    arrived = m3r[0]
    for k in range(1, ngx):
        arrived = arrived + m3r[k]
    heat = WALL_RATIO * arrived[2:4]
    flux = heat * arrived[0:2]
    is_wall, is_cool = srow == 0, srow == layers - 1
    bound = jnp.where(is_wall, per_block(heat[0:1], heat[1:2]), jnp.where(is_cool, COOL, 0.0))
    source = jnp.where(is_wall, per_block(flux[0:1], flux[1:2]), jnp.where(is_cool, COOL * cool_at, 0.0))
    inverse = 1.0 / (c_up + c_dn + c_lf + c_rt + bound)
    for _ in range(SWEEPS):
        total = c_up * pltpu.roll(temps, 1, 0) + c_dn * pltpu.roll(temps, lines - 1, 0)
        total = total + c_lf * pltpu.roll(temps, 1, 1) + c_rt * pltpu.roll(temps, width - 1, 1)
        temps = (total + source) * inverse
    surf[me] = jnp.concatenate([temps[0:1], temps[layers : layers + 1]], axis=0)

    def send_surface(k, carry):
        dev = lax.rem(me + k, ndev)
        pltpu.make_async_remote_copy(
            src_ref=surf.at[me], dst_ref=surf.at[me], send_sem=gs.at[4], recv_sem=gr.at[4],
            device_id=(dev // ngy, lax.rem(dev, ngy)), device_id_type=MESH,
        ).start()
        return carry

    lax.fori_loop(1, ndev, send_surface, 0)
    solid_ref[...] = temps.reshape(2, layers, width)

    for group in (wy, wx, vy, vx, ys, xt, xk, xu, y1, x1):
        group[2]()
    all_in(cbuf, ngx, gs.at[0])
    all_in(cc, ngy, gs.at[1])
    all_in(nb, ngy, gs.at[2])
    all_in(m3r, ngx, gs.at[3])
    all_in(surf, ndev, gs.at[4])

    all_in(surf, ndev, gr.at[4])
    back = jnp.dot(fetch[:, :ndev], surf[:, 0, :], precision=EXACT, preferred_element_type=F32)
    back = back + jnp.dot(fetch[:, ndev:], surf[:, 1, :], precision=EXACT, preferred_element_type=F32)
    per = 128 // ny
    lines_out = []
    shifted = [back if s == 0 else pltpu.roll(back, 128 - s * ny, 1) for s in range(per)]
    for x in range(nx):
        lines_out.append(shifted[x % per][x // per : x // per + 1, 0:ny])
    full = jnp.concatenate(lines_out, axis=0)
    is_live = iota((nx, ny), 0) // per < count_ref[0]
    wallout_ref[...] = jnp.where(is_live, full, wall_ref[...])


def solution(mesh):
    ngx, ngy = mesh.shape["gx"], mesh.shape["gy"]

    def shards(temp, kappa, vel, wall, count, fmap, stemp, scond, cool):
        nx, ny, nz = temp.shape
        cells, ndev = nx * ny, ngx * ngy
        vmem = pl.BlockSpec(memory_space=pltpu.VMEM)
        hbm = pl.BlockSpec(memory_space=pl.ANY)
        padded = (nx + 2, ny + 2 * PAD, nz)
        dma = pltpu.SemaphoreType.DMA
        out = pl.pallas_call(
            functools.partial(kernel, ngx, ngy),
            out_shape=(
                jax.ShapeDtypeStruct(temp.shape, F32),
                jax.ShapeDtypeStruct(wall.shape, F32),
                jax.ShapeDtypeStruct(stemp.shape, F32),
            ),
            in_specs=[hbm, hbm, hbm, vmem, pl.BlockSpec(memory_space=pltpu.SMEM), vmem, vmem, vmem, vmem],
            out_specs=(vmem, vmem, vmem),
            scratch_shapes=[
                pltpu.VMEM(padded, F32),
                pltpu.VMEM(padded, F32),
                pltpu.VMEM(padded, F32),
                pltpu.VMEM((nx + 2, ny, nz), F32),
                pltpu.VMEM((nx, ny + 2 * PAD, nz), F32),
                pltpu.VMEM((nx, ny, nz), F32),
                pltpu.VMEM((7, nx, ny, nz), F32),
                pltpu.VMEM((nx, ny, nz), jnp.bfloat16),
                pltpu.VMEM((3, nx, ny, nz), jnp.bfloat16),
                pltpu.VMEM((nx, ny, 128), F32),
                pltpu.VMEM((2, 3, nx, 1, nz), F32),
                pltpu.VMEM((2, 3, nx, 1, nz), F32),
                pltpu.VMEM((2, nx, 1, nz), F32),
                pltpu.VMEM((2, nx, 1, nz), F32),
                pltpu.VMEM((8, cells), F32),
                pltpu.VMEM((2, 8, cells), F32),
                pltpu.VMEM((2, 8, 128), F32),
                pltpu.VMEM((2, 8, 128), F32),
                pltpu.VMEM((8, cells), F32),
                pltpu.VMEM((2, 8, cells), F32),
                pltpu.VMEM((2, 8, 128), F32),
                pltpu.VMEM((2, 8, 128), F32),
                pltpu.VMEM((ngx, 8, 128), F32),
                pltpu.VMEM((8, 128), F32),
                pltpu.VMEM((ngy, 16, 128), F32),
                pltpu.VMEM((ngy, 8, 128), F32),
                pltpu.VMEM((ngx, 8, 128), F32),
                pltpu.VMEM((ngx, 8, 128), F32),
                pltpu.VMEM((ndev, 2, 128), F32),
                dma((3,)),
                dma((4, 2)),
                dma((4, 2)),
                dma((2, 2)),
                dma((2, 2)),
                dma((2, 2)),
                dma((2, 2)),
                dma((2, 2)),
                dma((2, 2)),
                dma((5,)),
                dma((5,)),
                dma((1,)),
                pltpu.SemaphoreType.REGULAR((3,)),
            ],
            compiler_params=pltpu.CompilerParams(
                collective_id=0, has_side_effects=True, vmem_limit_bytes=60 << 20
            ),
            name="coupled_step",
        )(temp, kappa, vel, wall, count, fmap.reshape(1, -1), stemp, scond, cool)
        return out

    return jax.shard_map(
        shards,
        mesh=mesh,
        in_specs=(
            P("gx", "gy", None),
            P("gx", "gy", None),
            P(None, "gx", "gy", None),
            P("gx", "gy"),
            P(("gx", "gy")),
            P(),
            P(("gx", "gy"), None, None),
            P(("gx", "gy"), None, None),
            P(("gx", "gy"), None),
        ),
        out_specs=(P("gx", "gy", None), P("gx", "gy"), P(("gx", "gy"), None, None)),
        check_vma=False,
    )
```

```python
import functools

import jax
import jax.numpy as jnp
from jax import lax
from jax.experimental import pallas as pl
from jax.experimental.pallas import tpu as pltpu
from jax.sharding import PartitionSpec as P

MESH = pl.DeviceIdType.MESH
F32 = jnp.float32
SWEEPS = 6
WALL_RATIO = 25.0
COOL = 1.0
EXACT = lax.Precision.HIGHEST
PAD = 8


def nt_dot(a, b, precision=None):
    return lax.dot_general(
        a, b, (((1,), (1,)), ((), ())), precision=precision, preferred_element_type=F32
    )


def iota(shape, axis):
    return lax.broadcasted_iota(jnp.int32, shape, axis)


def slab_step(temp, k0, ux, uy, uz, wall, t_nb, k_nb, u_nb):
    rows = temp.shape[0]
    row = iota(temp.shape, 0)
    out = temp
    for pos, (sign, own) in enumerate(((1, ux), (-1, ux), (1, uy), (-1, uy))):
        kk, uu, n = k0 + k_nb[pos], own + u_nb[pos], t_nb[pos]
        out = out + kk * (n - temp) - sign * uu * (temp + n)
    up = pltpu.roll(temp, rows - 1, 0)
    kk, uu = k0 + pltpu.roll(k0, rows - 1, 0), uz + pltpu.roll(uz, rows - 1, 0)
    out = out + kk * (up - temp) - uu * (temp + up)
    first = row == 0
    down = jnp.where(first, wall, pltpu.roll(temp, 1, 0))
    kk = k0 + jnp.where(first, 0.0, pltpu.roll(k0, 1, 0))
    uu = uz + jnp.where(first, 0.0, pltpu.roll(uz, 1, 0))
    return out + kk * (down - temp) + uu * (temp + down)


def conductances(conds, layers):
    lines, width = conds.shape
    row, col = lax.rem(iota(conds.shape, 0), layers), iota(conds.shape, 1)
    up = jnp.where(row == 0, 0.0, 0.5 * (conds + pltpu.roll(conds, 1, 0)))
    down = jnp.where(row == layers - 1, 0.0, 0.5 * (conds + pltpu.roll(conds, lines - 1, 0)))
    left = jnp.where(col == 0, 0.0, 0.5 * (conds + pltpu.roll(conds, 1, 1)))
    right = jnp.where(col == width - 1, 0.0, 0.5 * (conds + pltpu.roll(conds, width - 1, 1)))
    return up, down, left, right


def sweep(temps, up, down, left, right, source, inverse):
    lines, width = temps.shape
    total = up * pltpu.roll(temps, 1, 0) + down * pltpu.roll(temps, lines - 1, 0)
    total = total + left * pltpu.roll(temps, 1, 1) + right * pltpu.roll(temps, width - 1, 1)
    return (total + source) * inverse


def kernel(
    ngx, ngy,
    t_hbm, k_hbm, v_hbm, wall_ref, count_ref, map_ref, st_ref, sc_ref, cool_ref,
    fluid_ref, wallout_ref, solid_ref,
    tp, t1p, kp, uxp, uyp, uzp, coef, kraw, vraw, wallb,
    ys_send, ys_recv, y1_send, y1_recv,
    wy_send, wy_recv, wx_send, wx_recv, vy_send, vy_recv, vx_send, vx_recv,
    cbuf, csend, cc, nb, m3s, m3r, tops, m5s, m5r,
    ld_sem, hs, hr, t1s, t1r, ws, wr, v2s, v2r, gs, gr,
):
    nx, ny, nz = t_hbm.shape
    cells = nx * ny
    nblk = cells // 128
    ndev = ngx * ngy
    nsolid = 2 * ndev
    i, j = lax.axis_index("gx"), lax.axis_index("gy")
    me = i * ngy + j

    def gxd(k):
        return (lax.rem(i + k + ngx, ngx), j)

    def gyd(k):
        return (i, lax.rem(j + k + ngy, ngy))

    barrier = pltpu.get_barrier_semaphore()
    peers = [gxd(k) for k in range(1, ngx)] + [gyd(k) for k in range(1, ngy)]
    for peer in peers:
        pl.semaphore_signal(barrier, inc=1, device_id=peer, device_id_type=MESH)
    loads = []
    for part, zs in enumerate((pl.ds(0, 128), pl.ds(128, nz - 128))):
        inside = (pl.ds(1, nx), pl.ds(PAD, ny), zs)
        loads.append((
            pltpu.make_async_copy(t_hbm.at[:, :, zs], tp.at[inside], ld_sem.at[0, part]),
            pltpu.make_async_copy(k_hbm.at[:, :, zs], kraw.at[:, :, zs], ld_sem.at[1, part]),
            pltpu.make_async_copy(v_hbm.at[:, :, :, zs], vraw.at[:, :, :, zs], ld_sem.at[2, part]),
        ))
    for group in loads:
        for load in group:
            load.start()

    eye = iota((ny, ny), 0) == iota((ny, ny), 1)

    def wall_body(x, carry):
        line = wall_ref[pl.ds(x, 1), :]
        col = jnp.sum(jnp.where(eye, jnp.broadcast_to(line, (ny, ny)), 0.0), axis=1, keepdims=True)
        wallb[x] = jnp.broadcast_to(col, (ny, 128))
        return carry

    lax.fori_loop(0, nx, wall_body, 0)

    for cond, plane in ((i == 0, 0), (i == ngx - 1, nx + 1)):

        @pl.when(cond)
        def _():
            tp[plane] = jnp.zeros(tp.shape[1:], F32)
            t1p[plane] = jnp.zeros(t1p.shape[1:], F32)
            kp[plane] = jnp.zeros(kp.shape[1:], F32)
            uxp[plane] = jnp.zeros(uxp.shape[1:], F32)
            side = 0 if plane == 0 else 1
            wx_recv[side] = jnp.zeros(wx_recv.shape[1:], F32)
            vx_recv[side] = jnp.zeros(vx_recv.shape[1:], F32)

    for cond, side in ((j == 0, 0), (j == ngy - 1, 1)):

        @pl.when(cond)
        def _():
            ys_recv[side] = jnp.zeros(ys_recv.shape[1:], F32)
            y1_recv[side] = jnp.zeros(y1_recv.shape[1:], F32)
            wy_recv[side] = jnp.zeros(wy_recv.shape[1:], F32)
            vy_recv[side] = jnp.zeros(vy_recv.shape[1:], F32)

    s_w = jnp.concatenate([wall_ref[x : x + 1, :] for x in range(nx)], axis=1)

    def halo(src_of, dst_of, send, recv, axis):
        def make(up):
            spot, size, dev = (i, ngx, gxd) if axis == 0 else (j, ngy, gyd)
            copy = pltpu.make_async_remote_copy(
                src_ref=src_of(up), dst_ref=dst_of(up),
                send_sem=send.at[up], recv_sem=recv.at[up],
                device_id=dev(1 if up else -1), device_id_type=MESH,
            )
            sends = spot < size - 1 if up else spot > 0
            gets = spot > 0 if up else spot < size - 1
            return copy, sends, gets

        pairs = [make(1), make(0)]

        def start():
            for copy, sends, gets in pairs:
                pl.when(sends)(copy.start)

        def wait_recv():
            for copy, sends, gets in pairs:
                pl.when(gets)(copy.wait_recv)

        def wait_send():
            for copy, sends, gets in pairs:
                pl.when(sends)(copy.wait_send)

        return start, wait_recv, wait_send

    wy = halo(lambda up: wy_send, lambda up: wy_recv.at[1 - up], ws.at[0], wr.at[0], 1)
    wx = halo(lambda up: wx_send.at[up], lambda up: wx_recv.at[1 - up], ws.at[1], wr.at[1], 0)
    vy = halo(lambda up: vy_send, lambda up: vy_recv.at[1 - up], v2s.at[0], v2r.at[0], 1)
    vx = halo(lambda up: vx_send.at[up], lambda up: vx_recv.at[1 - up], v2s.at[1], v2r.at[1], 0)
    ys = halo(lambda up: ys_send.at[up], lambda up: ys_recv.at[1 - up], hs.at[0], hr.at[0], 1)

    def planes(ref, padded):
        rows = pl.ds(PAD, ny) if padded else pl.ds(0, ny)
        return (
            lambda up: ref.at[nx if up else 1, rows],
            lambda up: ref.at[0 if up else nx + 1, rows],
        )

    xt = halo(*planes(tp, True), hs.at[1], hr.at[1], 0)
    xk = halo(*planes(kp, True), hs.at[2], hr.at[2], 0)
    xu = halo(*planes(uxp, False), hs.at[3], hr.at[3], 0)
    y1 = halo(lambda up: y1_send.at[up], lambda up: y1_recv.at[1 - up], t1s.at[0], t1r.at[0], 1)
    x1 = halo(*planes(t1p, True), t1s.at[1], t1r.at[1], 0)

    for load in loads[0]:
        load.wait()

    counts = jnp.full((8, 128), count_ref[0], jnp.int32).astype(F32)
    csend[...] = counts
    tops[i, 0:16] = st_ref[:, 0:8].reshape(16, 128)
    tops[i, 16:32] = sc_ref[:, 0:8].reshape(16, 128)

    def spread(src, buf, slot, size, dev, sem, rsem):
        for k in range(1, size):
            pltpu.make_async_remote_copy(
                src_ref=src(k), dst_ref=buf.at[slot], send_sem=sem, recv_sem=rsem,
                device_id=dev(k), device_id_type=MESH,
            ).start()

    def all_in(buf, size, sem):
        part = buf.at[pl.ds(0, size - 1)]
        pltpu.make_async_copy(part, part, sem).wait()


    pick16 = (iota((8, 128), 0) == iota((8, 128), 1)).astype(F32).astype(jnp.bfloat16)

    def slab(value):
        return nt_dot(pick16, value.reshape(cells, 128))

    rest = tp[1 : nx + 1, PAD : PAD + ny, 0:128].reshape(cells, 128)
    s_t = jnp.zeros((8, cells), F32)
    for _ in range(3):
        piece = rest.astype(jnp.bfloat16)
        s_t = s_t + nt_dot(pick16, piece)
        rest = rest - piece.astype(F32)
    s_k = 0.5 * slab(kraw[:, :, 0:128])
    s_ux = 0.25 * slab(vraw[0, :, :, 0:128])
    s_uy = 0.25 * slab(vraw[1, :, :, 0:128])
    s_uz = 0.25 * slab(vraw[2, :, :, 0:128])
    wy_send[0:2, :] = s_t[0:2]
    wy_send[2:4, :] = s_k[0:2]
    wy_send[4:6, :] = s_uy[0:2]
    wy_send[6:8, :] = jnp.zeros((2, cells), F32)
    for up, lanes in ((1, slice(cells - 128, cells)), (0, slice(0, 128))):
        wx_send[up, 0:2, :] = s_t[0:2, lanes]
        wx_send[up, 2:4, :] = s_k[0:2, lanes]
        wx_send[up, 4:6, :] = s_ux[0:2, lanes]
        wx_send[up, 6:8, :] = jnp.zeros((2, 128), F32)
    pl.semaphore_wait(barrier, len(peers))
    wy[0]()
    wx[0]()
    spread(lambda k: csend, cbuf, i, ngx, gxd, gs.at[0], gr.at[0])
    spread(lambda k: tops.at[i], tops, i, ngx, gxd, gs.at[4], gr.at[4])
    for load in loads[1]:
        load.wait()

    def convert(x, carry):
        kv = 0.5 * kraw[x].astype(F32)
        kp[x + 1, PAD : PAD + ny, :] = kv
        uxp[x + 1] = 0.25 * vraw[0, x].astype(F32)
        uv = 0.25 * vraw[1, x].astype(F32)
        uyp[x, PAD : PAD + ny, :] = uv
        uzp[x] = 0.25 * vraw[2, x].astype(F32)
        ys_send[0, 0, x] = tp[x + 1, PAD : PAD + 1, :]
        ys_send[1, 0, x] = tp[x + 1, PAD + ny - 1 : PAD + ny, :]
        ys_send[0, 1, x] = kv[0:1]
        ys_send[1, 1, x] = kv[ny - 1 : ny]
        ys_send[0, 2, x] = uv[0:1]
        ys_send[1, 2, x] = uv[ny - 1 : ny]
        return carry

    lax.fori_loop(0, nx, convert, 0, unroll=4)
    ys[0]()
    xk[0]()
    xu[0]()
    xt[0]()

    lane = iota((8, cells), 1)
    y_first, y_last = lax.rem(lane, ny) == 0, lax.rem(lane, ny) == ny - 1
    x_first, x_last = lane < ny, lane >= cells - ny

    def y_neighbours(own, low, high):
        plus = jnp.where(y_last, pltpu.roll(high, ny - 1, 1), pltpu.roll(own, cells - 1, 1))
        minus = jnp.where(y_first, pltpu.roll(low, cells - (ny - 1), 1), pltpu.roll(own, 1, 1))
        return plus, minus

    def widen(tile):
        return jnp.concatenate([tile] * (cells // 128), axis=1)

    def x_neighbours(own, low, high):
        plus = jnp.where(x_last, widen(pltpu.roll(high, 128 - ny, 1)), pltpu.roll(own, cells - ny, 1))
        minus = jnp.where(x_first, widen(pltpu.roll(low, ny, 1)), pltpu.roll(own, ny, 1))
        return plus, minus

    wy[1]()
    wx[1]()

    def rows_of(value, part):
        return pltpu.roll(value, 8 - 2 * part, 0) if part else value

    ylow, yhigh, xlow, xhigh = wy_recv[0], wy_recv[1], wx_recv[0], wx_recv[1]
    ty = y_neighbours(s_t, rows_of(ylow, 0), rows_of(yhigh, 0))
    ky = y_neighbours(s_k, rows_of(ylow, 1), rows_of(yhigh, 1))
    uy = y_neighbours(s_uy, rows_of(ylow, 2), rows_of(yhigh, 2))
    tx = x_neighbours(s_t, rows_of(xlow, 0), rows_of(xhigh, 0))
    kx = x_neighbours(s_k, rows_of(xlow, 1), rows_of(xhigh, 1))
    ux = x_neighbours(s_ux, rows_of(xlow, 2), rows_of(xhigh, 2))
    k_nb, u_nb = kx + ky, ux + uy
    first = slab_step(s_t, s_k, s_ux, s_uy, s_uz, s_w, tx + ty, k_nb, u_nb)
    vy_send[...] = first
    vx_send[1] = first[:, cells - 128 :]
    vx_send[0] = first[:, 0:128]
    vy[0]()
    vx[0]()

    cbuf[i] = counts
    cond_blocks = jnp.concatenate([s_k[0:1, 128 * b : 128 * b + 128] for b in range(nblk)], axis=0)
    all_in(cbuf, ngx, gr.at[0])
    row8 = iota((8, 128), 0)
    column = jnp.zeros((8, 128), F32)
    for k in range(ngx):
        column = column + jnp.where(row8 == k, cbuf[k], 0.0)
    cc[j, 0:8] = cond_blocks
    cc[j, 8:16] = column
    spread(lambda k: cc.at[j], cc, j, ngy, gyd, gs.at[1], gr.at[1])

    vy[1]()
    vx[1]()
    ty = y_neighbours(first, vy_recv[0], vy_recv[1])
    tx = x_neighbours(first, vx_recv[0], vx_recv[1])
    second = slab_step(first, s_k, s_ux, s_uy, s_uz, s_w, tx + ty, k_nb, u_nb)
    nb[j] = jnp.concatenate([second[0:1, 128 * b : 128 * b + 128] for b in range(nblk)], axis=0)
    spread(lambda k: nb.at[j], nb, j, ngy, gyd, gs.at[2], gr.at[2])

    ys[1]()
    xk[1]()
    xu[1]()
    zlane = iota((8, nz), 1)
    z_first, z_last = zlane == 0, zlane == nz - 1

    def coef_body(x, carry):
        kp[x + 1, PAD - 1 : PAD, :] = ys_recv[0, 1, x]
        kp[x + 1, PAD + ny : PAD + ny + 1, :] = ys_recv[1, 1, x]
        uyp[x, PAD - 1 : PAD, :] = ys_recv[0, 2, x]
        uyp[x, PAD + ny : PAD + ny + 1, :] = ys_recv[1, 2, x]
        tp[x + 1, PAD - 1 : PAD, :] = ys_recv[0, 0, x]
        tp[x + 1, PAD + ny : PAD + ny + 1, :] = ys_recv[1, 0, x]
        for yt in range(0, ny, 8):
            y0 = PAD + yt
            k0 = kp[x + 1, y0 : y0 + 8, :]
            ux0 = uxp[x + 1, yt : yt + 8, :]
            uy0 = uyp[x, y0 : y0 + 8, :]
            uz0 = uzp[x, yt : yt + 8, :]
            here = pl.ds(yt, 8)
            kk, uu = k0 + kp[x + 2, y0 : y0 + 8, :], ux0 + uxp[x + 2, yt : yt + 8, :]
            coef[1, x, here] = kk - uu
            total = kk + uu
            kk, uu = k0 + kp[x, y0 : y0 + 8, :], ux0 + uxp[x, yt : yt + 8, :]
            coef[2, x, here] = kk + uu
            total = total + (kk - uu)
            kk, uu = k0 + kp[x + 1, y0 + 1 : y0 + 9, :], uy0 + uyp[x, y0 + 1 : y0 + 9, :]
            coef[3, x, here] = kk - uu
            total = total + (kk + uu)
            kk, uu = k0 + kp[x + 1, y0 - 1 : y0 + 7, :], uy0 + uyp[x, y0 - 1 : y0 + 7, :]
            coef[4, x, here] = kk + uu
            total = total + (kk - uu)
            kk = k0 + jnp.where(z_last, 0.0, pltpu.roll(k0, nz - 1, 1))
            uu = uz0 + jnp.where(z_last, 0.0, pltpu.roll(uz0, nz - 1, 1))
            coef[5, x, here] = jnp.where(z_last, 0.0, kk - uu)
            total = total + (kk + uu)
            kk = k0 + jnp.where(z_first, 0.0, pltpu.roll(k0, 1, 1))
            uu = uz0 + jnp.where(z_first, 0.0, pltpu.roll(uz0, 1, 1))
            coef[6, x, here] = kk + uu
            total = total + (kk - uu)
            coef[0, x, here] = 1.0 - total
        return carry

    lax.fori_loop(0, nx, coef_body, 0, unroll=4)

    def step_at(src, x, yt):
        y0 = PAD + yt
        here = pl.ds(yt, 8)
        mid = src[x + 1, y0 : y0 + 8, :]
        wall = jnp.concatenate([wallb[x, here]] * (nz // 128), axis=1)
        down = jnp.where(z_first, wall, pltpu.roll(mid, 1, 1))
        out = coef[0, x, here] * mid
        out = out + coef[1, x, here] * src[x + 2, y0 : y0 + 8, :]
        out = out + coef[2, x, here] * src[x, y0 : y0 + 8, :]
        out = out + coef[3, x, here] * src[x + 1, y0 + 1 : y0 + 9, :]
        out = out + coef[4, x, here] * src[x + 1, y0 - 1 : y0 + 7, :]
        out = out + coef[5, x, here] * pltpu.roll(mid, nz - 1, 1)
        return out + coef[6, x, here] * down

    xt[1]()

    def first_body(x, carry):
        for yt in range(0, ny, 8):
            value = step_at(tp, x, yt)
            t1p[x + 1, PAD + yt : PAD + yt + 8, :] = value
            if yt == 0:
                y1_send[0, x] = value[0:1]
            if yt == ny - 8:
                y1_send[1, x] = value[7:8]
        return carry

    lax.fori_loop(0, nx, first_body, 0, unroll=4)
    y1[0]()
    x1[0]()

    all_in(cc, ngy, gr.at[1])
    q = iota((8, 128), 1)
    table = jnp.zeros((8, 128), F32)
    for k in range(ngy):
        table = table + jnp.where(q // nblk == k, cc[k, 8:16], 0.0)
    before = (iota((128, 128), 0) // nblk < iota((128, 128), 1) // nblk).astype(F32) * (1.0 / nblk)
    prefix = jnp.dot(table, before, precision=EXACT, preferred_element_type=F32)
    row_total = jnp.sum(table, axis=1, keepdims=True) * (1.0 / nblk)
    offset = jnp.sum(
        jnp.where(row8 == i, prefix, 0.0) + jnp.where(row8 < i, jnp.broadcast_to(row_total, (8, 128)), 0.0),
        axis=0, keepdims=True,
    )
    mine = jnp.sum(jnp.where(row8 == i, table, 0.0), axis=0, keepdims=True)
    slot = lax.rem(iota((1, 128), 1), nblk).astype(F32)
    live = slot < mine
    rank = jnp.where(live, offset + slot, -1.0)
    onehot = (iota((nsolid, 128), 0).astype(F32) == rank).astype(F32)
    fmap = map_ref[...].astype(F32)
    target = jnp.dot(fmap, onehot, precision=EXACT, preferred_element_type=F32)
    target = jnp.where(live, target, -1.0)
    line = iota((8 * ngx, 128), 0)
    kind = lax.rem(line, 8)
    owner = 2 * ((line // 8) * ngy + j)
    for_near = jnp.where(kind < 2, owner + kind, -2).astype(F32)
    for_cond = jnp.where((kind >= 2) & (kind < 4), owner + kind - 2, -2).astype(F32)
    w_near = (for_near == target).astype(F32)
    w_cond = (for_cond == target).astype(F32)
    cond_rows = cc[:, 0:8].reshape(128, 128)
    payload_c = jnp.dot(w_cond, cond_rows, precision=EXACT, preferred_element_type=F32)

    top_line = iota((128, 128), 0)
    top_row = lax.rem(top_line, 8)
    top_block = top_line // 8
    top_id = jnp.where(top_row == 0, 2 * ((top_block // 2) * ngy + j) + lax.rem(top_block, 2), -2)
    w_top = (top_id.astype(F32) == target).astype(F32)
    w_back = jnp.transpose(w_top)
    all_in(tops, ngx, gr.at[4])
    top_t = tops[:, 0:16].reshape(128, 128)
    top_c = tops[:, 16:32].reshape(128, 128)
    top_up, top_dn, top_lf, top_rt = conductances(top_c, 8)
    top_bound = WALL_RATIO * jnp.dot(w_top, cond_rows, precision=EXACT, preferred_element_type=F32)
    top_inv = 1.0 / (top_up + top_dn + top_lf + top_rt + top_bound)

    all_in(nb, ngy, gr.at[2])
    near_rows = nb[...].reshape(128, 128)
    payload = payload_c + jnp.dot(w_near, near_rows, precision=EXACT, preferred_element_type=F32)
    m3s[...] = payload.reshape(ngx, 8, 128)
    spread(lambda k: m3s.at[gxd(k)[0]], m3r, i, ngx, gxd, gs.at[3], gr.at[3])
    m3r[i] = m3s[i]
    top_src = top_bound * jnp.dot(w_top, near_rows, precision=EXACT, preferred_element_type=F32)
    for _ in range(SWEEPS):
        top_t = sweep(top_t, top_up, top_dn, top_lf, top_rt, top_src, top_inv)
    m5s[...] = jnp.dot(w_back, top_t, precision=EXACT, preferred_element_type=F32).reshape(ngy, 8, 128)
    spread(lambda k: m5s.at[gyd(k)[1]], m5r, j, ngy, gyd, gs.at[5], gr.at[5])
    m5r[j] = m5s[j]

    layers, width = st_ref.shape[1:]
    lines = 2 * layers
    temps = st_ref[...].reshape(lines, width)
    srow = lax.rem(iota((lines, width), 0), layers)
    c_up, c_dn, c_lf, c_rt = conductances(sc_ref[...].reshape(lines, width), layers)
    cool = cool_ref[...]

    def per_block(a, b):
        return jnp.concatenate(
            [jnp.broadcast_to(a, (layers, width)), jnp.broadcast_to(b, (layers, width))], axis=0
        )

    cool_at = per_block(cool[0:1], cool[1:2])

    all_in(m3r, ngx, gr.at[3])
    arrived = m3r[0]
    for k in range(1, ngx):
        arrived = arrived + m3r[k]
    heat = WALL_RATIO * arrived[2:4]
    flux = heat * arrived[0:2]
    is_wall, is_cool = srow == 0, srow == layers - 1
    bound = jnp.where(is_wall, per_block(heat[0:1], heat[1:2]), jnp.where(is_cool, COOL, 0.0))
    source = jnp.where(is_wall, per_block(flux[0:1], flux[1:2]), jnp.where(is_cool, COOL * cool_at, 0.0))
    inverse = 1.0 / (c_up + c_dn + c_lf + c_rt + bound)
    for _ in range(SWEEPS):
        temps = sweep(temps, c_up, c_dn, c_lf, c_rt, source, inverse)
    solid_ref[...] = temps.reshape(2, layers, width)

    y1[1]()
    x1[1]()

    def second_body(x, carry):
        t1p[x + 1, PAD - 1 : PAD, :] = y1_recv[0, x]
        t1p[x + 1, PAD + ny : PAD + ny + 1, :] = y1_recv[1, x]
        for yt in range(0, ny, 8):
            fluid_ref[x, pl.ds(yt, 8)] = step_at(t1p, x, yt)
        return carry

    lax.fori_loop(0, nx, second_body, 0, unroll=4)

    for group in (wy, wx, vy, vx, ys, xt, xk, xu, y1, x1):
        group[2]()
    all_in(cbuf, ngx, gs.at[0])
    all_in(cc, ngy, gs.at[1])
    all_in(nb, ngy, gs.at[2])
    all_in(m3r, ngx, gs.at[3])
    all_in(tops, ngx, gs.at[4])
    all_in(m5r, ngy, gs.at[5])

    all_in(m5r, ngy, gr.at[5])
    back = m5r[0]
    for k in range(1, ngy):
        back = back + m5r[k]
    per = 128 // ny
    lines_out = []
    shifted = [back if s == 0 else pltpu.roll(back, 128 - s * ny, 1) for s in range(per)]
    for x in range(nx):
        lines_out.append(shifted[x % per][x // per : x // per + 1, 0:ny])
    full = jnp.concatenate(lines_out, axis=0)
    is_live = iota((nx, ny), 0) // per < count_ref[0]
    wallout_ref[...] = jnp.where(is_live, full, wall_ref[...])


def finish(fluid, wall, solid, fluid_ref, wall_ref, solid_ref, sem):
    copies = [
        pltpu.make_async_copy(src, dst, sem.at[n])
        for n, (src, dst) in enumerate(((fluid, fluid_ref), (wall, wall_ref), (solid, solid_ref)))
    ]
    for copy in copies:
        copy.start()
    for copy in copies:
        copy.wait()


def solution(mesh):
    ngx, ngy = mesh.shape["gx"], mesh.shape["gy"]

    def shards(temp, kappa, vel, wall, count, fmap, stemp, scond, cool):
        nx, ny, nz = temp.shape
        cells, ndev = nx * ny, ngx * ngy
        vmem = pl.BlockSpec(memory_space=pltpu.VMEM)
        hbm = pl.BlockSpec(memory_space=pl.ANY)
        padded = (nx + 2, ny + 2 * PAD, nz)
        dma = pltpu.SemaphoreType.DMA
        out = pl.pallas_call(
            functools.partial(kernel, ngx, ngy),
            out_shape=(
                pltpu.VMEM(temp.shape, F32),
                pltpu.VMEM(wall.shape, F32),
                pltpu.VMEM(stemp.shape, F32),
            ),
            in_specs=[hbm, hbm, hbm, vmem, pl.BlockSpec(memory_space=pltpu.SMEM), vmem, vmem, vmem, vmem],
            out_specs=(vmem, vmem, vmem),
            scratch_shapes=[
                pltpu.VMEM(padded, F32),
                pltpu.VMEM(padded, F32),
                pltpu.VMEM(padded, F32),
                pltpu.VMEM((nx + 2, ny, nz), F32),
                pltpu.VMEM((nx, ny + 2 * PAD, nz), F32),
                pltpu.VMEM((nx, ny, nz), F32),
                pltpu.VMEM((7, nx, ny, nz), F32),
                pltpu.VMEM((nx, ny, nz), jnp.bfloat16),
                pltpu.VMEM((3, nx, ny, nz), jnp.bfloat16),
                pltpu.VMEM((nx, ny, 128), F32),
                pltpu.VMEM((2, 3, nx, 1, nz), F32),
                pltpu.VMEM((2, 3, nx, 1, nz), F32),
                pltpu.VMEM((2, nx, 1, nz), F32),
                pltpu.VMEM((2, nx, 1, nz), F32),
                pltpu.VMEM((8, cells), F32),
                pltpu.VMEM((2, 8, cells), F32),
                pltpu.VMEM((2, 8, 128), F32),
                pltpu.VMEM((2, 8, 128), F32),
                pltpu.VMEM((8, cells), F32),
                pltpu.VMEM((2, 8, cells), F32),
                pltpu.VMEM((2, 8, 128), F32),
                pltpu.VMEM((2, 8, 128), F32),
                pltpu.VMEM((ngx, 8, 128), F32),
                pltpu.VMEM((8, 128), F32),
                pltpu.VMEM((ngy, 16, 128), F32),
                pltpu.VMEM((ngy, 8, 128), F32),
                pltpu.VMEM((ngx, 8, 128), F32),
                pltpu.VMEM((ngx, 8, 128), F32),
                pltpu.VMEM((ngx, 32, 128), F32),
                pltpu.VMEM((ngy, 8, 128), F32),
                pltpu.VMEM((ngy, 8, 128), F32),
                dma((3, 2)),
                dma((4, 2)),
                dma((4, 2)),
                dma((2, 2)),
                dma((2, 2)),
                dma((2, 2)),
                dma((2, 2)),
                dma((2, 2)),
                dma((2, 2)),
                dma((6,)),
                dma((6,)),
            ],
            compiler_params=pltpu.CompilerParams(
                collective_id=0, has_side_effects=True, vmem_limit_bytes=60 << 20
            ),
            name="coupled_step",
        )(temp, kappa, vel, wall, count, fmap.reshape(1, -1), stemp, scond, cool)
        return pl.pallas_call(
            finish,
            out_shape=(
                jax.ShapeDtypeStruct(temp.shape, F32),
                jax.ShapeDtypeStruct(wall.shape, F32),
                jax.ShapeDtypeStruct(stemp.shape, F32),
            ),
            in_specs=[vmem] * 3,
            out_specs=(hbm,) * 3,
            scratch_shapes=[dma((3,))],
            compiler_params=pltpu.CompilerParams(vmem_limit_bytes=1 << 20),
            name="write_out",
        )(*[pltpu.with_memory_space_constraint(o, pltpu.VMEM) for o in out])

    return jax.shard_map(
        shards,
        mesh=mesh,
        in_specs=(
            P("gx", "gy", None),
            P("gx", "gy", None),
            P(None, "gx", "gy", None),
            P("gx", "gy"),
            P(("gx", "gy")),
            P(),
            P(("gx", "gy"), None, None),
            P(("gx", "gy"), None, None),
            P(("gx", "gy"), None),
        ),
        out_specs=(P("gx", "gy", None), P("gx", "gy"), P(("gx", "gy"), None, None)),
        check_vma=False,
    )
```

```python
import functools

import jax
import jax.numpy as jnp
from jax import lax
from jax.experimental import pallas as pl
from jax.experimental.pallas import tpu as pltpu
from jax.sharding import PartitionSpec as P

MESH = pl.DeviceIdType.MESH
F32 = jnp.float32
SWEEPS = 6
WALL_RATIO = 25.0
COOL = 1.0
EXACT = lax.Precision.HIGHEST
PAD = 8


def nt_dot(a, b, precision=None):
    return lax.dot_general(
        a, b, (((1,), (1,)), ((), ())), precision=precision, preferred_element_type=F32
    )


def iota(shape, axis):
    return lax.broadcasted_iota(jnp.int32, shape, axis)


def thirds(value):
    pieces = []
    for _ in range(3):
        piece = value.astype(jnp.bfloat16)
        pieces.append(piece)
        value = value - piece.astype(F32)
    return pieces


def pick_rows(onehot, pieces):
    return sum(jnp.dot(onehot, piece, preferred_element_type=F32) for piece in pieces)


def slab_step(temp, k0, ux, uy, uz, wall, t_nb, k_nb, u_nb):
    rows = temp.shape[0]
    row = iota(temp.shape, 0)
    out = temp
    for pos, (sign, own) in enumerate(((1, ux), (-1, ux), (1, uy), (-1, uy))):
        kk, uu, n = k0 + k_nb[pos], own + u_nb[pos], t_nb[pos]
        out = out + kk * (n - temp) - sign * uu * (temp + n)
    up = pltpu.roll(temp, rows - 1, 0)
    kk, uu = k0 + pltpu.roll(k0, rows - 1, 0), uz + pltpu.roll(uz, rows - 1, 0)
    out = out + kk * (up - temp) - uu * (temp + up)
    first = row == 0
    down = jnp.where(first, wall, pltpu.roll(temp, 1, 0))
    kk = k0 + jnp.where(first, 0.0, pltpu.roll(k0, 1, 0))
    uu = uz + jnp.where(first, 0.0, pltpu.roll(uz, 1, 0))
    return out + kk * (down - temp) + uu * (temp + down)


def conductances(conds, layers):
    lines, width = conds.shape
    row, col = lax.rem(iota(conds.shape, 0), layers), iota(conds.shape, 1)
    up = jnp.where(row == 0, 0.0, 0.5 * (conds + pltpu.roll(conds, 1, 0)))
    down = jnp.where(row == layers - 1, 0.0, 0.5 * (conds + pltpu.roll(conds, lines - 1, 0)))
    left = jnp.where(col == 0, 0.0, 0.5 * (conds + pltpu.roll(conds, 1, 1)))
    right = jnp.where(col == width - 1, 0.0, 0.5 * (conds + pltpu.roll(conds, width - 1, 1)))
    return up, down, left, right


def sweep(temps, up, down, left, right, source, inverse):
    lines, width = temps.shape
    total = up * pltpu.roll(temps, 1, 0) + down * pltpu.roll(temps, lines - 1, 0)
    total = total + left * pltpu.roll(temps, 1, 1) + right * pltpu.roll(temps, width - 1, 1)
    return (total + source) * inverse


def kernel(
    ngx, ngy,
    t_hbm, k_hbm, v_hbm, wall_ref, count_ref, map_ref, st_ref, sc_ref, cool_ref,
    fluid_ref, wallout_ref, solid_ref,
    tp, t1p, kp, uxp, uyp, uzp, coef, kraw, vraw, wallb,
    ys_send, ys_recv, y1_send, y1_recv,
    wy_send, wy_recv, wx_send, wx_recv, vy_send, vy_recv, vx_send, vx_recv,
    cbuf, csend, cc, nb, m3s, m3r, tops, m5s, m5r,
    ld_sem, hs, hr, t1s, t1r, ws, wr, v2s, v2r, gs, gr,
):
    nx, ny, nz = t_hbm.shape
    cells = nx * ny
    nblk = cells // 128
    ndev = ngx * ngy
    nsolid = 2 * ndev
    i, j = lax.axis_index("gx"), lax.axis_index("gy")
    me = i * ngy + j

    def gxd(k):
        return (lax.rem(i + k + ngx, ngx), j)

    def gyd(k):
        return (i, lax.rem(j + k + ngy, ngy))

    barrier = pltpu.get_barrier_semaphore()
    peers = [gxd(k) for k in range(1, ngx)] + [gyd(k) for k in range(1, ngy)]
    for peer in peers:
        pl.semaphore_signal(barrier, inc=1, device_id=peer, device_id_type=MESH)
    loads = []
    for part, zs in enumerate((pl.ds(0, 128), pl.ds(128, nz - 128))):
        inside = (pl.ds(1, nx), pl.ds(PAD, ny), zs)
        loads.append((
            pltpu.make_async_copy(t_hbm.at[:, :, zs], tp.at[inside], ld_sem.at[0, part]),
            pltpu.make_async_copy(k_hbm.at[:, :, zs], kraw.at[:, :, zs], ld_sem.at[1, part]),
            pltpu.make_async_copy(v_hbm.at[:, :, :, zs], vraw.at[:, :, :, zs], ld_sem.at[2, part]),
        ))
    for group in loads:
        for load in group:
            load.start()

    eye = iota((ny, ny), 0) == iota((ny, ny), 1)

    def wall_body(x, carry):
        line = wall_ref[pl.ds(x, 1), :]
        col = jnp.sum(jnp.where(eye, jnp.broadcast_to(line, (ny, ny)), 0.0), axis=1, keepdims=True)
        wallb[x] = jnp.broadcast_to(col, (ny, 128))
        return carry

    lax.fori_loop(0, nx, wall_body, 0)

    for cond, plane in ((i == 0, 0), (i == ngx - 1, nx + 1)):

        @pl.when(cond)
        def _():
            tp[plane] = jnp.zeros(tp.shape[1:], F32)
            t1p[plane] = jnp.zeros(t1p.shape[1:], F32)
            kp[plane] = jnp.zeros(kp.shape[1:], F32)
            uxp[plane] = jnp.zeros(uxp.shape[1:], F32)
            side = 0 if plane == 0 else 1
            wx_recv[side] = jnp.zeros(wx_recv.shape[1:], F32)
            vx_recv[side] = jnp.zeros(vx_recv.shape[1:], F32)

    for cond, side in ((j == 0, 0), (j == ngy - 1, 1)):

        @pl.when(cond)
        def _():
            ys_recv[side] = jnp.zeros(ys_recv.shape[1:], F32)
            y1_recv[side] = jnp.zeros(y1_recv.shape[1:], F32)
            wy_recv[side] = jnp.zeros(wy_recv.shape[1:], F32)
            vy_recv[side] = jnp.zeros(vy_recv.shape[1:], F32)

    s_w = jnp.concatenate([wall_ref[x : x + 1, :] for x in range(nx)], axis=1)

    def halo(src_of, dst_of, send, recv, axis):
        def make(up):
            spot, size, dev = (i, ngx, gxd) if axis == 0 else (j, ngy, gyd)
            copy = pltpu.make_async_remote_copy(
                src_ref=src_of(up), dst_ref=dst_of(up),
                send_sem=send.at[up], recv_sem=recv.at[up],
                device_id=dev(1 if up else -1), device_id_type=MESH,
            )
            sends = spot < size - 1 if up else spot > 0
            gets = spot > 0 if up else spot < size - 1
            return copy, sends, gets

        pairs = [make(1), make(0)]

        def start():
            for copy, sends, gets in pairs:
                pl.when(sends)(copy.start)

        def wait_recv():
            for copy, sends, gets in pairs:
                pl.when(gets)(copy.wait_recv)

        def wait_send():
            for copy, sends, gets in pairs:
                pl.when(sends)(copy.wait_send)

        return start, wait_recv, wait_send

    wy = halo(lambda up: wy_send, lambda up: wy_recv.at[1 - up], ws.at[0], wr.at[0], 1)
    wx = halo(lambda up: wx_send.at[up], lambda up: wx_recv.at[1 - up], ws.at[1], wr.at[1], 0)
    vy = halo(lambda up: vy_send, lambda up: vy_recv.at[1 - up], v2s.at[0], v2r.at[0], 1)
    vx = halo(lambda up: vx_send.at[up], lambda up: vx_recv.at[1 - up], v2s.at[1], v2r.at[1], 0)
    ys = halo(lambda up: ys_send.at[up], lambda up: ys_recv.at[1 - up], hs.at[0], hr.at[0], 1)

    def planes(ref, padded):
        rows = pl.ds(PAD, ny) if padded else pl.ds(0, ny)
        return (
            lambda up: ref.at[nx if up else 1, rows],
            lambda up: ref.at[0 if up else nx + 1, rows],
        )

    xt = halo(*planes(tp, True), hs.at[1], hr.at[1], 0)
    xk = halo(*planes(kp, True), hs.at[2], hr.at[2], 0)
    xu = halo(*planes(uxp, False), hs.at[3], hr.at[3], 0)
    y1 = halo(lambda up: y1_send.at[up], lambda up: y1_recv.at[1 - up], t1s.at[0], t1r.at[0], 1)
    x1 = halo(*planes(t1p, True), t1s.at[1], t1r.at[1], 0)

    for load in loads[0]:
        load.wait()

    counts = jnp.full((8, 128), count_ref[0], jnp.int32).astype(F32)
    csend[...] = counts
    tops[i, 0:16] = st_ref[:, 0:8].reshape(16, 128)
    tops[i, 16:32] = sc_ref[:, 0:8].reshape(16, 128)

    def spread(src, buf, slot, size, dev, sem, rsem):
        for k in range(1, size):
            pltpu.make_async_remote_copy(
                src_ref=src(k), dst_ref=buf.at[slot], send_sem=sem, recv_sem=rsem,
                device_id=dev(k), device_id_type=MESH,
            ).start()

    def all_in(buf, size, sem):
        part = buf.at[pl.ds(0, size - 1)]
        pltpu.make_async_copy(part, part, sem).wait()


    pick16 = (iota((8, 128), 0) == iota((8, 128), 1)).astype(F32).astype(jnp.bfloat16)

    def slab(value):
        return nt_dot(pick16, value.reshape(cells, 128))

    s_t = sum(nt_dot(pick16, piece) for piece in thirds(tp[1 : nx + 1, PAD : PAD + ny, 0:128].reshape(cells, 128)))
    s_k = 0.5 * slab(kraw[:, :, 0:128])
    s_ux = 0.25 * slab(vraw[0, :, :, 0:128])
    s_uy = 0.25 * slab(vraw[1, :, :, 0:128])
    s_uz = 0.25 * slab(vraw[2, :, :, 0:128])
    wy_send[0:2, :] = s_t[0:2]
    wy_send[2:4, :] = s_k[0:2]
    wy_send[4:6, :] = s_uy[0:2]
    wy_send[6:8, :] = jnp.zeros((2, cells), F32)
    for up, lanes in ((1, slice(cells - 128, cells)), (0, slice(0, 128))):
        wx_send[up, 0:2, :] = s_t[0:2, lanes]
        wx_send[up, 2:4, :] = s_k[0:2, lanes]
        wx_send[up, 4:6, :] = s_ux[0:2, lanes]
        wx_send[up, 6:8, :] = jnp.zeros((2, 128), F32)
    pl.semaphore_wait(barrier, len(peers))
    spread(lambda k: csend, cbuf, i, ngx, gxd, gs.at[0], gr.at[0])
    wy[0]()
    wx[0]()
    for load in loads[1]:
        load.wait()

    def convert(x, carry):
        kv = 0.5 * kraw[x].astype(F32)
        kp[x + 1, PAD : PAD + ny, :] = kv
        uxp[x + 1] = 0.25 * vraw[0, x].astype(F32)
        uv = 0.25 * vraw[1, x].astype(F32)
        uyp[x, PAD : PAD + ny, :] = uv
        uzp[x] = 0.25 * vraw[2, x].astype(F32)
        ys_send[0, 0, x] = tp[x + 1, PAD : PAD + 1, :]
        ys_send[1, 0, x] = tp[x + 1, PAD + ny - 1 : PAD + ny, :]
        ys_send[0, 1, x] = kv[0:1]
        ys_send[1, 1, x] = kv[ny - 1 : ny]
        ys_send[0, 2, x] = uv[0:1]
        ys_send[1, 2, x] = uv[ny - 1 : ny]
        return carry

    lax.fori_loop(0, nx, convert, 0, unroll=4)
    ys[0]()
    xk[0]()
    xu[0]()
    xt[0]()

    lane = iota((8, cells), 1)
    y_first, y_last = lax.rem(lane, ny) == 0, lax.rem(lane, ny) == ny - 1
    x_first, x_last = lane < ny, lane >= cells - ny

    def y_neighbours(own, low, high):
        plus = jnp.where(y_last, pltpu.roll(high, ny - 1, 1), pltpu.roll(own, cells - 1, 1))
        minus = jnp.where(y_first, pltpu.roll(low, cells - (ny - 1), 1), pltpu.roll(own, 1, 1))
        return plus, minus

    def widen(tile):
        return jnp.concatenate([tile] * (cells // 128), axis=1)

    def x_neighbours(own, low, high):
        plus = jnp.where(x_last, widen(pltpu.roll(high, 128 - ny, 1)), pltpu.roll(own, cells - ny, 1))
        minus = jnp.where(x_first, widen(pltpu.roll(low, ny, 1)), pltpu.roll(own, ny, 1))
        return plus, minus

    wy[1]()
    wx[1]()

    def rows_of(value, part):
        return pltpu.roll(value, 8 - 2 * part, 0) if part else value

    ylow, yhigh, xlow, xhigh = wy_recv[0], wy_recv[1], wx_recv[0], wx_recv[1]
    ty = y_neighbours(s_t, rows_of(ylow, 0), rows_of(yhigh, 0))
    ky = y_neighbours(s_k, rows_of(ylow, 1), rows_of(yhigh, 1))
    uy = y_neighbours(s_uy, rows_of(ylow, 2), rows_of(yhigh, 2))
    tx = x_neighbours(s_t, rows_of(xlow, 0), rows_of(xhigh, 0))
    kx = x_neighbours(s_k, rows_of(xlow, 1), rows_of(xhigh, 1))
    ux = x_neighbours(s_ux, rows_of(xlow, 2), rows_of(xhigh, 2))
    k_nb, u_nb = kx + ky, ux + uy
    first = slab_step(s_t, s_k, s_ux, s_uy, s_uz, s_w, tx + ty, k_nb, u_nb)
    vy_send[...] = first
    vx_send[1] = first[:, cells - 128 :]
    vx_send[0] = first[:, 0:128]
    vy[0]()
    vx[0]()

    cbuf[i] = counts
    cond_blocks = jnp.concatenate([s_k[0:1, 128 * b : 128 * b + 128] for b in range(nblk)], axis=0)
    all_in(cbuf, ngx, gr.at[0])
    row8 = iota((8, 128), 0)
    column = jnp.zeros((8, 128), F32)
    for k in range(ngx):
        column = column + jnp.where(row8 == k, cbuf[k], 0.0)
    cc[j, 0:8] = cond_blocks
    cc[j, 8:16] = column
    spread(lambda k: cc.at[j], cc, j, ngy, gyd, gs.at[1], gr.at[1])
    spread(lambda k: tops.at[i], tops, i, ngx, gxd, gs.at[4], gr.at[4])

    zlane = iota((8, nz), 1)
    z_first, z_last = zlane == 0, zlane == nz - 1

    def stencil(src, x, yt, co):
        y0 = PAD + yt
        mid = src[x + 1, y0 : y0 + 8, :]
        wall = jnp.concatenate([wallb[x, pl.ds(yt, 8)]] * (nz // 128), axis=1)
        down = jnp.where(z_first, wall, pltpu.roll(mid, 1, 1))
        out = co(0) * mid
        out = out + co(1) * src[x + 2, y0 : y0 + 8, :]
        out = out + co(2) * src[x, y0 : y0 + 8, :]
        out = out + co(3) * src[x + 1, y0 + 1 : y0 + 9, :]
        out = out + co(4) * src[x + 1, y0 - 1 : y0 + 7, :]
        out = out + co(5) * pltpu.roll(mid, nz - 1, 1)
        return out + co(6) * down

    def advance_first(x, yt):
        y0 = PAD + yt
        k0 = kp[x + 1, y0 : y0 + 8, :]
        ux0 = uxp[x + 1, yt : yt + 8, :]
        uy0 = uyp[x, y0 : y0 + 8, :]
        uz0 = uzp[x, yt : yt + 8, :]
        kk, uu = k0 + kp[x + 2, y0 : y0 + 8, :], ux0 + uxp[x + 2, yt : yt + 8, :]
        total, c1 = kk + uu, kk - uu
        kk, uu = k0 + kp[x, y0 : y0 + 8, :], ux0 + uxp[x, yt : yt + 8, :]
        total, c2 = total + (kk - uu), kk + uu
        kk, uu = k0 + kp[x + 1, y0 + 1 : y0 + 9, :], uy0 + uyp[x, y0 + 1 : y0 + 9, :]
        total, c3 = total + (kk + uu), kk - uu
        kk, uu = k0 + kp[x + 1, y0 - 1 : y0 + 7, :], uy0 + uyp[x, y0 - 1 : y0 + 7, :]
        total, c4 = total + (kk - uu), kk + uu
        low, high = k0 - uz0, k0 + uz0
        c5 = jnp.where(z_last, 0.0, low + pltpu.roll(low, nz - 1, 1))
        total = total + (high + jnp.where(z_last, 0.0, pltpu.roll(high, nz - 1, 1)))
        c6 = high + jnp.where(z_first, 0.0, pltpu.roll(high, 1, 1))
        total = total + (low + jnp.where(z_first, 0.0, pltpu.roll(low, 1, 1)))
        made = (1.0 - total, c1, c2, c3, c4, c5, c6)
        for n, value in enumerate(made):
            coef[n, x, pl.ds(yt, 8)] = value
        value = stencil(tp, x, yt, lambda n: made[n])
        t1p[x + 1, y0 : y0 + 8, :] = value
        return value

    middle = range(8, ny - 8, 8)

    def middle_body(x, carry):
        for yt in middle:
            advance_first(x, yt)
        return carry

    lax.fori_loop(1, nx - 1, middle_body, 0, unroll=5)

    vy[1]()
    vx[1]()
    ty = y_neighbours(first, vy_recv[0], vy_recv[1])
    tx = x_neighbours(first, vx_recv[0], vx_recv[1])
    second = slab_step(first, s_k, s_ux, s_uy, s_uz, s_w, tx + ty, k_nb, u_nb)
    nb[j] = jnp.concatenate([second[0:1, 128 * b : 128 * b + 128] for b in range(nblk)], axis=0)
    spread(lambda k: nb.at[j], nb, j, ngy, gyd, gs.at[2], gr.at[2])

    ys[1]()
    xk[1]()
    xu[1]()
    xt[1]()
    for x in (0, nx - 1):
        middle_body(x, 0)

    def edge_body(x, carry):
        for row, side in ((PAD - 1, 0), (PAD + ny, 1)):
            tp[x + 1, row : row + 1, :] = ys_recv[side, 0, x]
            kp[x + 1, row : row + 1, :] = ys_recv[side, 1, x]
            uyp[x, row : row + 1, :] = ys_recv[side, 2, x]
        y1_send[0, x] = advance_first(x, 0)[0:1]
        y1_send[1, x] = advance_first(x, ny - 8)[7:8]
        return carry

    lax.fori_loop(0, nx, edge_body, 0, unroll=4)
    y1[0]()
    x1[0]()

    all_in(cc, ngy, gr.at[1])
    q = iota((8, 128), 1)
    table = jnp.zeros((8, 128), F32)
    for k in range(ngy):
        table = table + jnp.where(q // nblk == k, cc[k, 8:16], 0.0)
    before = (iota((128, 128), 0) // nblk < iota((128, 128), 1) // nblk).astype(F32) * (1.0 / nblk)
    prefix = jnp.dot(table, before, precision=EXACT, preferred_element_type=F32)
    row_total = jnp.sum(table, axis=1, keepdims=True) * (1.0 / nblk)
    offset = jnp.sum(
        jnp.where(row8 == i, prefix, 0.0) + jnp.where(row8 < i, jnp.broadcast_to(row_total, (8, 128)), 0.0),
        axis=0, keepdims=True,
    )
    mine = jnp.sum(jnp.where(row8 == i, table, 0.0), axis=0, keepdims=True)
    slot = lax.rem(iota((1, 128), 1), nblk).astype(F32)
    live = slot < mine
    rank = jnp.where(live, offset + slot, -1.0)
    onehot = (iota((nsolid, 128), 0).astype(F32) == rank).astype(F32)
    fmap = map_ref[...].astype(F32)
    target = jnp.dot(fmap, onehot, precision=EXACT, preferred_element_type=F32)
    target = jnp.where(live, target, -1.0)
    line = iota((8 * ngx, 128), 0)
    kind = lax.rem(line, 8)
    owner = 2 * ((line // 8) * ngy + j)
    for_near = jnp.where(kind < 2, owner + kind, -2).astype(F32)
    for_cond = jnp.where((kind >= 2) & (kind < 4), owner + kind - 2, -2).astype(F32)
    w_near = (for_near == target).astype(F32).astype(jnp.bfloat16)
    w_cond = (for_cond == target).astype(F32).astype(jnp.bfloat16)
    cond_rows = thirds(cc[:, 0:8].reshape(128, 128))
    payload_c = pick_rows(w_cond, cond_rows)

    top_line = iota((128, 128), 0)
    top_row = lax.rem(top_line, 8)
    top_block = top_line // 8
    top_id = jnp.where(top_row == 0, 2 * ((top_block // 2) * ngy + j) + lax.rem(top_block, 2), -2)
    w_top = (top_id.astype(F32) == target).astype(F32)
    w_back = jnp.transpose(w_top).astype(jnp.bfloat16)
    w_top = w_top.astype(jnp.bfloat16)
    all_in(tops, ngx, gr.at[4])
    top_t = tops[:, 0:16].reshape(128, 128)
    top_c = tops[:, 16:32].reshape(128, 128)
    top_up, top_dn, top_lf, top_rt = conductances(top_c, 8)
    top_bound = WALL_RATIO * pick_rows(w_top, cond_rows)
    top_inv = 1.0 / (top_up + top_dn + top_lf + top_rt + top_bound)

    all_in(nb, ngy, gr.at[2])
    near_rows = thirds(nb[...].reshape(128, 128))
    payload = payload_c + pick_rows(w_near, near_rows)
    m3s[...] = payload.reshape(ngx, 8, 128)
    spread(lambda k: m3s.at[gxd(k)[0]], m3r, i, ngx, gxd, gs.at[3], gr.at[3])
    m3r[i] = m3s[i]
    top_src = top_bound * pick_rows(w_top, near_rows)
    for _ in range(SWEEPS):
        top_t = sweep(top_t, top_up, top_dn, top_lf, top_rt, top_src, top_inv)
    m5s[...] = pick_rows(w_back, thirds(top_t)).reshape(ngy, 8, 128)
    spread(lambda k: m5s.at[gyd(k)[1]], m5r, j, ngy, gyd, gs.at[5], gr.at[5])
    m5r[j] = m5s[j]

    layers, width = st_ref.shape[1:]
    lines = 2 * layers
    temps = st_ref[...].reshape(lines, width)
    srow = lax.rem(iota((lines, width), 0), layers)
    c_up, c_dn, c_lf, c_rt = conductances(sc_ref[...].reshape(lines, width), layers)
    cool = cool_ref[...]

    def per_block(a, b):
        return jnp.concatenate(
            [jnp.broadcast_to(a, (layers, width)), jnp.broadcast_to(b, (layers, width))], axis=0
        )

    cool_at = per_block(cool[0:1], cool[1:2])

    y1[1]()
    x1[1]()

    def second_body(x, carry):
        t1p[x + 1, PAD - 1 : PAD, :] = y1_recv[0, x]
        t1p[x + 1, PAD + ny : PAD + ny + 1, :] = y1_recv[1, x]
        for yt in range(0, ny, 8):
            fluid_ref[x, pl.ds(yt, 8)] = stencil(t1p, x, yt, lambda n: coef[n, x, pl.ds(yt, 8)])
        return carry

    lax.fori_loop(0, nx, second_body, 0, unroll=4)

    all_in(m3r, ngx, gr.at[3])
    arrived = m3r[0]
    for k in range(1, ngx):
        arrived = arrived + m3r[k]
    heat = WALL_RATIO * arrived[2:4]
    flux = heat * arrived[0:2]
    is_wall, is_cool = srow == 0, srow == layers - 1
    bound = jnp.where(is_wall, per_block(heat[0:1], heat[1:2]), jnp.where(is_cool, COOL, 0.0))
    source = jnp.where(is_wall, per_block(flux[0:1], flux[1:2]), jnp.where(is_cool, COOL * cool_at, 0.0))
    inverse = 1.0 / (c_up + c_dn + c_lf + c_rt + bound)
    for _ in range(SWEEPS):
        temps = sweep(temps, c_up, c_dn, c_lf, c_rt, source, inverse)
    solid_ref[...] = temps.reshape(2, layers, width)

    for group in (wy, wx, vy, vx, ys, xt, xk, xu, y1, x1):
        group[2]()
    all_in(cbuf, ngx, gs.at[0])
    all_in(cc, ngy, gs.at[1])
    all_in(nb, ngy, gs.at[2])
    all_in(m3r, ngx, gs.at[3])
    all_in(tops, ngx, gs.at[4])
    all_in(m5r, ngy, gs.at[5])

    all_in(m5r, ngy, gr.at[5])
    back = m5r[0]
    for k in range(1, ngy):
        back = back + m5r[k]
    per = 128 // ny
    lines_out = []
    shifted = [back if s == 0 else pltpu.roll(back, 128 - s * ny, 1) for s in range(per)]
    for x in range(nx):
        lines_out.append(shifted[x % per][x // per : x // per + 1, 0:ny])
    full = jnp.concatenate(lines_out, axis=0)
    is_live = iota((nx, ny), 0) // per < count_ref[0]
    wallout_ref[...] = jnp.where(is_live, full, wall_ref[...])


def finish(fluid, wall, solid, fluid_ref, wall_ref, solid_ref, sem):
    copies = [
        pltpu.make_async_copy(src, dst, sem.at[n])
        for n, (src, dst) in enumerate(((fluid, fluid_ref), (wall, wall_ref), (solid, solid_ref)))
    ]
    for copy in copies:
        copy.start()
    for copy in copies:
        copy.wait()


def solution(mesh):
    ngx, ngy = mesh.shape["gx"], mesh.shape["gy"]

    def shards(temp, kappa, vel, wall, count, fmap, stemp, scond, cool):
        nx, ny, nz = temp.shape
        cells, ndev = nx * ny, ngx * ngy
        vmem = pl.BlockSpec(memory_space=pltpu.VMEM)
        hbm = pl.BlockSpec(memory_space=pl.ANY)
        padded = (nx + 2, ny + 2 * PAD, nz)
        dma = pltpu.SemaphoreType.DMA
        out = pl.pallas_call(
            functools.partial(kernel, ngx, ngy),
            out_shape=(
                pltpu.VMEM(temp.shape, F32),
                pltpu.VMEM(wall.shape, F32),
                pltpu.VMEM(stemp.shape, F32),
            ),
            in_specs=[hbm, hbm, hbm, vmem, pl.BlockSpec(memory_space=pltpu.SMEM), vmem, vmem, vmem, vmem],
            out_specs=(vmem, vmem, vmem),
            scratch_shapes=[
                pltpu.VMEM(padded, F32),
                pltpu.VMEM(padded, F32),
                pltpu.VMEM(padded, F32),
                pltpu.VMEM((nx + 2, ny, nz), F32),
                pltpu.VMEM((nx, ny + 2 * PAD, nz), F32),
                pltpu.VMEM((nx, ny, nz), F32),
                pltpu.VMEM((7, nx, ny, nz), F32),
                pltpu.VMEM((nx, ny, nz), jnp.bfloat16),
                pltpu.VMEM((3, nx, ny, nz), jnp.bfloat16),
                pltpu.VMEM((nx, ny, 128), F32),
                pltpu.VMEM((2, 3, nx, 1, nz), F32),
                pltpu.VMEM((2, 3, nx, 1, nz), F32),
                pltpu.VMEM((2, nx, 1, nz), F32),
                pltpu.VMEM((2, nx, 1, nz), F32),
                pltpu.VMEM((8, cells), F32),
                pltpu.VMEM((2, 8, cells), F32),
                pltpu.VMEM((2, 8, 128), F32),
                pltpu.VMEM((2, 8, 128), F32),
                pltpu.VMEM((8, cells), F32),
                pltpu.VMEM((2, 8, cells), F32),
                pltpu.VMEM((2, 8, 128), F32),
                pltpu.VMEM((2, 8, 128), F32),
                pltpu.VMEM((ngx, 8, 128), F32),
                pltpu.VMEM((8, 128), F32),
                pltpu.VMEM((ngy, 16, 128), F32),
                pltpu.VMEM((ngy, 8, 128), F32),
                pltpu.VMEM((ngx, 8, 128), F32),
                pltpu.VMEM((ngx, 8, 128), F32),
                pltpu.VMEM((ngx, 32, 128), F32),
                pltpu.VMEM((ngy, 8, 128), F32),
                pltpu.VMEM((ngy, 8, 128), F32),
                dma((3, 2)),
                dma((4, 2)),
                dma((4, 2)),
                dma((2, 2)),
                dma((2, 2)),
                dma((2, 2)),
                dma((2, 2)),
                dma((2, 2)),
                dma((2, 2)),
                dma((6,)),
                dma((6,)),
            ],
            compiler_params=pltpu.CompilerParams(
                collective_id=0, has_side_effects=True, vmem_limit_bytes=60 << 20
            ),
            name="coupled_step",
        )(temp, kappa, vel, wall, count, fmap.reshape(1, -1), stemp, scond, cool)
        return pl.pallas_call(
            finish,
            out_shape=(
                jax.ShapeDtypeStruct(temp.shape, F32),
                jax.ShapeDtypeStruct(wall.shape, F32),
                jax.ShapeDtypeStruct(stemp.shape, F32),
            ),
            in_specs=[vmem] * 3,
            out_specs=(hbm,) * 3,
            scratch_shapes=[dma((3,))],
            compiler_params=pltpu.CompilerParams(vmem_limit_bytes=1 << 20),
            name="write_out",
        )(*[pltpu.with_memory_space_constraint(o, pltpu.VMEM) for o in out])

    return jax.shard_map(
        shards,
        mesh=mesh,
        in_specs=(
            P("gx", "gy", None),
            P("gx", "gy", None),
            P(None, "gx", "gy", None),
            P("gx", "gy"),
            P(("gx", "gy")),
            P(),
            P(("gx", "gy"), None, None),
            P(("gx", "gy"), None, None),
            P(("gx", "gy"), None),
        ),
        out_specs=(P("gx", "gy", None), P("gx", "gy"), P(("gx", "gy"), None, None)),
        check_vma=False,
    )
```

```python
import functools

import jax
import jax.numpy as jnp
from jax import lax
from jax.experimental import pallas as pl
from jax.experimental.pallas import tpu as pltpu
from jax.sharding import PartitionSpec as P

MESH = pl.DeviceIdType.MESH
F32 = jnp.float32
SWEEPS = 6
WALL_RATIO = 25.0
COOL = 1.0
EXACT = lax.Precision.HIGHEST
PAD = 8


def nt_dot(a, b, precision=None):
    return lax.dot_general(
        a, b, (((1,), (1,)), ((), ())), precision=precision, preferred_element_type=F32
    )


def iota(shape, axis):
    return lax.broadcasted_iota(jnp.int32, shape, axis)


def thirds(value):
    pieces = []
    for _ in range(3):
        piece = value.astype(jnp.bfloat16)
        pieces.append(piece)
        value = value - piece.astype(F32)
    return pieces


def pick_rows(onehot, pieces):
    return sum(jnp.dot(onehot, piece, preferred_element_type=F32) for piece in pieces)


def across(temp, k0, own, n, kn, un, sign):
    return (k0 + kn) * (n - temp) - sign * (own + un) * (temp + n)


def upright(temp, k0, uz, wall):
    rows = temp.shape[0]
    first = iota(temp.shape, 0) == 0

    def above(value):
        return pltpu.roll(value, rows - 1, 0)

    def below(value, ground):
        return jnp.where(first, ground, pltpu.roll(value, 1, 0))

    out = temp + across(temp, k0, uz, above(temp), above(k0), above(uz), 1.0)
    return out + across(temp, k0, uz, below(temp, wall), below(k0, 0.0), below(uz, 0.0), -1.0)


def conductances(conds, layers):
    lines, width = conds.shape
    row, col = lax.rem(iota(conds.shape, 0), layers), iota(conds.shape, 1)
    up = jnp.where(row == 0, 0.0, 0.5 * (conds + pltpu.roll(conds, 1, 0)))
    down = jnp.where(row == layers - 1, 0.0, 0.5 * (conds + pltpu.roll(conds, lines - 1, 0)))
    left = jnp.where(col == 0, 0.0, 0.5 * (conds + pltpu.roll(conds, 1, 1)))
    right = jnp.where(col == width - 1, 0.0, 0.5 * (conds + pltpu.roll(conds, width - 1, 1)))
    return up, down, left, right


def sweep(temps, up, down, left, right, source, inverse):
    lines, width = temps.shape
    total = up * pltpu.roll(temps, 1, 0) + down * pltpu.roll(temps, lines - 1, 0)
    total = total + left * pltpu.roll(temps, 1, 1) + right * pltpu.roll(temps, width - 1, 1)
    return (total + source) * inverse


def kernel(
    ngx, ngy,
    t_hbm, k_hbm, v_hbm, wall_ref, count_ref, map_ref, st_ref, sc_ref, cool_ref,
    fluid_ref, wallout_ref, solid_ref,
    tp, t1p, kp, uxp, uyp, uzp, coef, kraw, vraw, wallb,
    ys_send, ys_recv, y1_send, y1_recv,
    wy_send, wy_recv, wx_send, wx_recv, wd_recv,
    cbuf, csend, cc, nb, m3s, m3r, tops, m5s, m5r,
    ld_sem, hs, hr, t1s, t1r, ws, wr, wds, wdr, gs, gr,
):
    nx, ny, nz = t_hbm.shape
    cells = nx * ny
    nblk = cells // 128
    ndev = ngx * ngy
    nsolid = 2 * ndev
    i, j = lax.axis_index("gx"), lax.axis_index("gy")
    me = i * ngy + j

    def gxd(k):
        return (lax.rem(i + k + ngx, ngx), j)

    def gyd(k):
        return (i, lax.rem(j + k + ngy, ngy))

    barrier = pltpu.get_barrier_semaphore()
    peers = [gxd(k) for k in range(1, ngx)] + [gyd(k) for k in range(1, ngy)]
    peers += [(gxd(dx)[0], gyd(dy)[1]) for dx in (1, -1) for dy in (1, -1)]
    for peer in peers:
        pl.semaphore_signal(barrier, inc=1, device_id=peer, device_id_type=MESH)
    loads = []
    for part, zs in enumerate((pl.ds(0, 128), pl.ds(128, nz - 128))):
        inside = (pl.ds(1, nx), pl.ds(PAD, ny), zs)
        loads.append((
            pltpu.make_async_copy(t_hbm.at[:, :, zs], tp.at[inside], ld_sem.at[0, part]),
            pltpu.make_async_copy(k_hbm.at[:, :, zs], kraw.at[:, :, zs], ld_sem.at[1, part]),
            pltpu.make_async_copy(v_hbm.at[:, :, :, zs], vraw.at[:, :, :, zs], ld_sem.at[2, part]),
        ))
    for group in loads:
        for load in group:
            load.start()

    eye = iota((ny, ny), 0) == iota((ny, ny), 1)

    def wall_body(x, carry):
        line = wall_ref[pl.ds(x, 1), :]
        col = jnp.sum(jnp.where(eye, jnp.broadcast_to(line, (ny, ny)), 0.0), axis=1, keepdims=True)
        wallb[x] = jnp.broadcast_to(col, (ny, 128))
        return carry

    lax.fori_loop(0, nx, wall_body, 0)

    for cond, plane in ((i == 0, 0), (i == ngx - 1, nx + 1)):

        @pl.when(cond)
        def _():
            tp[plane] = jnp.zeros(tp.shape[1:], F32)
            t1p[plane] = jnp.zeros(t1p.shape[1:], F32)
            kp[plane] = jnp.zeros(kp.shape[1:], F32)
            uxp[plane] = jnp.zeros(uxp.shape[1:], F32)
            side = 0 if plane == 0 else 1
            wx_recv[side] = jnp.zeros(wx_recv.shape[1:], F32)
            wd_recv[side] = jnp.zeros(wd_recv.shape[1:], F32)

    for cond, side in ((j == 0, 0), (j == ngy - 1, 1)):

        @pl.when(cond)
        def _():
            ys_recv[side] = jnp.zeros(ys_recv.shape[1:], F32)
            y1_recv[side] = jnp.zeros(y1_recv.shape[1:], F32)
            wy_recv[side] = jnp.zeros(wy_recv.shape[1:], F32)
            wd_recv[:, side] = jnp.zeros((2, 8, 128), F32)

    s_w = jnp.concatenate([wall_ref[x : x + 1, :] for x in range(nx)], axis=1)

    def halo(src_of, dst_of, send, recv, axis):
        def make(up):
            spot, size, dev = (i, ngx, gxd) if axis == 0 else (j, ngy, gyd)
            copy = pltpu.make_async_remote_copy(
                src_ref=src_of(up), dst_ref=dst_of(up),
                send_sem=send.at[up], recv_sem=recv.at[up],
                device_id=dev(1 if up else -1), device_id_type=MESH,
            )
            sends = spot < size - 1 if up else spot > 0
            gets = spot > 0 if up else spot < size - 1
            return copy, sends, gets

        pairs = [make(1), make(0)]

        def start():
            for copy, sends, gets in pairs:
                pl.when(sends)(copy.start)

        def wait_recv():
            for copy, sends, gets in pairs:
                pl.when(gets)(copy.wait_recv)

        def wait_send():
            for copy, sends, gets in pairs:
                pl.when(sends)(copy.wait_send)

        return start, wait_recv, wait_send

    wy = halo(lambda up: wy_send, lambda up: wy_recv.at[1 - up], ws.at[0], wr.at[0], 1)
    wx = halo(lambda up: wx_send.at[up], lambda up: wx_recv.at[1 - up], ws.at[1], wr.at[1], 0)
    corners = []
    for upx in (0, 1):
        for upy in (0, 1):
            copy = pltpu.make_async_remote_copy(
                src_ref=wx_send.at[upx], dst_ref=wd_recv.at[1 - upx, 1 - upy],
                send_sem=wds.at[upx, upy], recv_sem=wdr.at[upx, upy],
                device_id=(gxd(1 if upx else -1)[0], gyd(1 if upy else -1)[1]), device_id_type=MESH,
            )
            low_x, high_x, low_y, high_y = i > 0, i < ngx - 1, j > 0, j < ngy - 1
            sends = jnp.logical_and(high_x if upx else low_x, high_y if upy else low_y)
            gets = jnp.logical_and(low_x if upx else high_x, low_y if upy else high_y)
            corners.append((copy, sends, gets))
    ys = halo(lambda up: ys_send.at[up], lambda up: ys_recv.at[1 - up], hs.at[0], hr.at[0], 1)

    def planes(ref, padded):
        rows = pl.ds(PAD, ny) if padded else pl.ds(0, ny)
        return (
            lambda up: ref.at[nx if up else 1, rows],
            lambda up: ref.at[0 if up else nx + 1, rows],
        )

    xt = halo(*planes(tp, True), hs.at[1], hr.at[1], 0)
    xk = halo(*planes(kp, True), hs.at[2], hr.at[2], 0)
    xu = halo(*planes(uxp, False), hs.at[3], hr.at[3], 0)
    y1 = halo(lambda up: y1_send.at[up], lambda up: y1_recv.at[1 - up], t1s.at[0], t1r.at[0], 1)
    x1 = halo(*planes(t1p, True), t1s.at[1], t1r.at[1], 0)

    for load in loads[0]:
        load.wait()

    counts = jnp.full((8, 128), count_ref[0], jnp.int32).astype(F32)
    csend[...] = counts
    tops[i, 0:16] = st_ref[:, 0:8].reshape(16, 128)
    tops[i, 16:32] = sc_ref[:, 0:8].reshape(16, 128)

    def spread(src, buf, slot, size, dev, sem, rsem):
        for k in range(1, size):
            pltpu.make_async_remote_copy(
                src_ref=src(k), dst_ref=buf.at[slot], send_sem=sem, recv_sem=rsem,
                device_id=dev(k), device_id_type=MESH,
            ).start()

    def all_in(buf, size, sem):
        part = buf.at[pl.ds(0, size - 1)]
        pltpu.make_async_copy(part, part, sem).wait()


    pick16 = (iota((8, 128), 0) == iota((8, 128), 1)).astype(F32).astype(jnp.bfloat16)

    def slab(value):
        return nt_dot(pick16, value.reshape(cells, 128))

    s_t = sum(nt_dot(pick16, piece) for piece in thirds(tp[1 : nx + 1, PAD : PAD + ny, 0:128].reshape(cells, 128)))
    s_k = 0.5 * slab(kraw[:, :, 0:128])
    s_ux = 0.25 * slab(vraw[0, :, :, 0:128])
    s_uy = 0.25 * slab(vraw[1, :, :, 0:128])
    s_uz = 0.25 * slab(vraw[2, :, :, 0:128])
    lane = iota((8, cells), 1)
    y_first, y_last = lax.rem(lane, ny) == 0, lax.rem(lane, ny) == ny - 1
    x_first, x_last = lane < ny, lane >= cells - ny
    partial = upright(s_t, s_k, s_uz, s_w)
    for shift, edge, own, sign in (
        (cells - ny, x_last, s_ux, 1.0), (ny, x_first, s_ux, -1.0),
        (cells - 1, y_last, s_uy, 1.0), (1, y_first, s_uy, -1.0),
    ):
        term = across(
            s_t, s_k, own, pltpu.roll(s_t, shift, 1), pltpu.roll(s_k, shift, 1), pltpu.roll(own, shift, 1), sign
        )
        partial = partial + jnp.where(edge, 0.0, term)
    wy_send[...] = jnp.concatenate([s_t[0:2], s_k[0:2], s_uy[0:2], partial[0:1], s_ux[0:1]], axis=0)
    for up, lanes in ((1, slice(cells - 128, cells)), (0, slice(0, 128))):
        wx_send[up] = jnp.concatenate(
            [s_t[0:2, lanes], s_k[0:2, lanes], s_ux[0:2, lanes], partial[0:1, lanes], s_uy[0:1, lanes]], axis=0
        )
    pl.semaphore_wait(barrier, len(peers))
    spread(lambda k: csend, cbuf, i, ngx, gxd, gs.at[0], gr.at[0])
    wy[0]()
    wx[0]()
    for copy, sends, gets in corners:
        pl.when(sends)(copy.start)
    for load in loads[1]:
        load.wait()

    def convert(x, carry):
        kv = 0.5 * kraw[x].astype(F32)
        kp[x + 1, PAD : PAD + ny, :] = kv
        uxp[x + 1] = 0.25 * vraw[0, x].astype(F32)
        uv = 0.25 * vraw[1, x].astype(F32)
        uyp[x, PAD : PAD + ny, :] = uv
        uzp[x] = 0.25 * vraw[2, x].astype(F32)
        ys_send[0, 0, x] = tp[x + 1, PAD : PAD + 1, :]
        ys_send[1, 0, x] = tp[x + 1, PAD + ny - 1 : PAD + ny, :]
        ys_send[0, 1, x] = kv[0:1]
        ys_send[1, 1, x] = kv[ny - 1 : ny]
        ys_send[0, 2, x] = uv[0:1]
        ys_send[1, 2, x] = uv[ny - 1 : ny]
        return carry

    lax.fori_loop(0, nx, convert, 0, unroll=4)
    ys[0]()
    xk[0]()
    xu[0]()
    xt[0]()

    zlane = iota((8, nz), 1)
    z_first, z_last = zlane == 0, zlane == nz - 1

    def stencil(src, x, yt, co):
        y0 = PAD + yt
        mid = src[x + 1, y0 : y0 + 8, :]
        wall = jnp.concatenate([wallb[x, pl.ds(yt, 8)]] * (nz // 128), axis=1)
        down = jnp.where(z_first, wall, pltpu.roll(mid, 1, 1))
        out = co(0) * mid
        out = out + co(1) * src[x + 2, y0 : y0 + 8, :]
        out = out + co(2) * src[x, y0 : y0 + 8, :]
        out = out + co(3) * src[x + 1, y0 + 1 : y0 + 9, :]
        out = out + co(4) * src[x + 1, y0 - 1 : y0 + 7, :]
        out = out + co(5) * pltpu.roll(mid, nz - 1, 1)
        return out + co(6) * down

    def advance_first(x, yt):
        y0 = PAD + yt
        k0 = kp[x + 1, y0 : y0 + 8, :]
        ux0 = uxp[x + 1, yt : yt + 8, :]
        uy0 = uyp[x, y0 : y0 + 8, :]
        uz0 = uzp[x, yt : yt + 8, :]
        kk, uu = k0 + kp[x + 2, y0 : y0 + 8, :], ux0 + uxp[x + 2, yt : yt + 8, :]
        total, c1 = kk + uu, kk - uu
        kk, uu = k0 + kp[x, y0 : y0 + 8, :], ux0 + uxp[x, yt : yt + 8, :]
        total, c2 = total + (kk - uu), kk + uu
        kk, uu = k0 + kp[x + 1, y0 + 1 : y0 + 9, :], uy0 + uyp[x, y0 + 1 : y0 + 9, :]
        total, c3 = total + (kk + uu), kk - uu
        kk, uu = k0 + kp[x + 1, y0 - 1 : y0 + 7, :], uy0 + uyp[x, y0 - 1 : y0 + 7, :]
        total, c4 = total + (kk - uu), kk + uu
        low, high = k0 - uz0, k0 + uz0
        c5 = jnp.where(z_last, 0.0, low + pltpu.roll(low, nz - 1, 1))
        total = total + (high + jnp.where(z_last, 0.0, pltpu.roll(high, nz - 1, 1)))
        c6 = high + jnp.where(z_first, 0.0, pltpu.roll(high, 1, 1))
        total = total + (low + jnp.where(z_first, 0.0, pltpu.roll(low, 1, 1)))
        made = (1.0 - total, c1, c2, c3, c4, c5, c6)
        for n, value in enumerate(made):
            coef[n, x, pl.ds(yt, 8)] = value
        value = stencil(tp, x, yt, lambda n: made[n])
        t1p[x + 1, y0 : y0 + 8, :] = value
        return value

    middle = range(8, ny - 8, 8)

    def middle_body(x, carry):
        for yt in middle:
            advance_first(x, yt)
        return carry

    lax.fori_loop(1, nx - 1, middle_body, 0, unroll=5)

    cbuf[i] = counts
    cond_blocks = jnp.concatenate([s_k[0:1, 128 * b : 128 * b + 128] for b in range(nblk)], axis=0)
    all_in(cbuf, ngx, gr.at[0])
    row8 = iota((8, 128), 0)
    column = jnp.zeros((8, 128), F32)
    for k in range(ngx):
        column = column + jnp.where(row8 == k, cbuf[k], 0.0)
    cc[j, 0:8] = cond_blocks
    cc[j, 8:16] = column
    spread(lambda k: cc.at[j], cc, j, ngy, gyd, gs.at[1], gr.at[1])
    spread(lambda k: tops.at[i], tops, i, ngx, gxd, gs.at[4], gr.at[4])

    def widen(tile):
        return jnp.concatenate([tile] * (cells // 128), axis=1)

    def row_first(value, row):
        return pltpu.roll(value, 8 - row, 0) if row else value

    wy[1]()
    wx[1]()
    for copy, sends, gets in corners:
        pl.when(gets)(copy.wait_recv)
    diag = {
        (sx, sy): pltpu.roll(wd_recv[sx, sy], shift, 1)
        for sx, sy, shift in ((0, 0, 1), (1, 0, 128 - ny + 1 - ny), (0, 1, 2 * ny - 1), (1, 1, 127))
    }
    first = partial
    beside = []
    for edge, seen, own, shift, sign, along, side, there in (
        (x_last, widen(pltpu.roll(wx_recv[1], 128 - ny, 1)), s_ux, cells - ny, 1.0, "x", 1, i < ngx - 1),
        (x_first, widen(pltpu.roll(wx_recv[0], ny, 1)), s_ux, ny, -1.0, "x", 0, i > 0),
        (y_last, pltpu.roll(wy_recv[1], ny - 1, 1), s_uy, cells - 1, 1.0, "y", 1, j < ngy - 1),
        (y_first, pltpu.roll(wy_recv[0], cells - (ny - 1), 1), s_uy, 1, -1.0, "y", 0, j > 0),
    ):
        n, kn, un = seen, row_first(seen, 2), row_first(seen, 4)
        term = across(s_t, s_k, own, n, kn, un, sign)
        first = first + jnp.where(edge, term, 0.0)
        beyond = row_first(seen, 6) - term
        cross = row_first(seen, 7)
        for other in (0, 1):
            d = widen(diag[(side, other)] if along == "x" else diag[(other, side)])
            ends = (y_last if other else y_first) if along == "x" else (x_last if other else x_first)
            d_u = row_first(d, 7 if along == "x" else 4)
            corner = across(n, kn, cross, d, row_first(d, 2), d_u, 1.0 if other else -1.0)
            beyond = beyond + jnp.where(ends, corner, 0.0)
        beyond = beyond * there.astype(F32)
        k_side = jnp.where(edge, kn, pltpu.roll(s_k, shift, 1))
        u_side = jnp.where(edge, un, pltpu.roll(own, shift, 1))
        beside.append((edge, beyond, own, shift, sign, k_side, u_side))
    second = upright(first, s_k, s_uz, s_w)
    for edge, beyond, own, shift, sign, k_side, u_side in beside:
        n = jnp.where(edge, beyond, pltpu.roll(first, shift, 1))
        second = second + across(first, s_k, own, n, k_side, u_side, sign)
    nb[j] = jnp.concatenate([second[0:1, 128 * b : 128 * b + 128] for b in range(nblk)], axis=0)
    spread(lambda k: nb.at[j], nb, j, ngy, gyd, gs.at[2], gr.at[2])

    ys[1]()
    xk[1]()
    xu[1]()
    xt[1]()
    for x in (0, nx - 1):
        middle_body(x, 0)

    def edge_body(x, carry):
        for row, side in ((PAD - 1, 0), (PAD + ny, 1)):
            tp[x + 1, row : row + 1, :] = ys_recv[side, 0, x]
            kp[x + 1, row : row + 1, :] = ys_recv[side, 1, x]
            uyp[x, row : row + 1, :] = ys_recv[side, 2, x]
        y1_send[0, x] = advance_first(x, 0)[0:1]
        y1_send[1, x] = advance_first(x, ny - 8)[7:8]
        return carry

    lax.fori_loop(0, nx, edge_body, 0, unroll=4)
    y1[0]()
    x1[0]()

    all_in(cc, ngy, gr.at[1])
    q = iota((8, 128), 1)
    table = jnp.zeros((8, 128), F32)
    for k in range(ngy):
        table = table + jnp.where(q // nblk == k, cc[k, 8:16], 0.0)
    before = (iota((128, 128), 0) // nblk < iota((128, 128), 1) // nblk).astype(F32) * (1.0 / nblk)
    prefix = jnp.dot(table, before, precision=EXACT, preferred_element_type=F32)
    row_total = jnp.sum(table, axis=1, keepdims=True) * (1.0 / nblk)
    offset = jnp.sum(
        jnp.where(row8 == i, prefix, 0.0) + jnp.where(row8 < i, jnp.broadcast_to(row_total, (8, 128)), 0.0),
        axis=0, keepdims=True,
    )
    mine = jnp.sum(jnp.where(row8 == i, table, 0.0), axis=0, keepdims=True)
    slot = lax.rem(iota((1, 128), 1), nblk).astype(F32)
    live = slot < mine
    rank = jnp.where(live, offset + slot, -1.0)
    onehot = (iota((nsolid, 128), 0).astype(F32) == rank).astype(F32)
    fmap = map_ref[...].astype(F32)
    target = jnp.dot(fmap, onehot, precision=EXACT, preferred_element_type=F32)
    target = jnp.where(live, target, -1.0)
    line = iota((8 * ngx, 128), 0)
    kind = lax.rem(line, 8)
    owner = 2 * ((line // 8) * ngy + j)
    for_near = jnp.where(kind < 2, owner + kind, -2).astype(F32)
    for_cond = jnp.where((kind >= 2) & (kind < 4), owner + kind - 2, -2).astype(F32)
    w_near = (for_near == target).astype(F32).astype(jnp.bfloat16)
    w_cond = (for_cond == target).astype(F32).astype(jnp.bfloat16)
    cond_rows = thirds(cc[:, 0:8].reshape(128, 128))
    payload_c = pick_rows(w_cond, cond_rows)

    top_line = iota((128, 128), 0)
    top_row = lax.rem(top_line, 8)
    top_block = top_line // 8
    top_id = jnp.where(top_row == 0, 2 * ((top_block // 2) * ngy + j) + lax.rem(top_block, 2), -2)
    w_top = (top_id.astype(F32) == target).astype(F32)
    w_back = jnp.transpose(w_top).astype(jnp.bfloat16)
    w_top = w_top.astype(jnp.bfloat16)
    all_in(tops, ngx, gr.at[4])
    top_t = tops[:, 0:16].reshape(128, 128)
    top_c = tops[:, 16:32].reshape(128, 128)
    top_up, top_dn, top_lf, top_rt = conductances(top_c, 8)
    top_bound = WALL_RATIO * pick_rows(w_top, cond_rows)
    top_inv = 1.0 / (top_up + top_dn + top_lf + top_rt + top_bound)

    all_in(nb, ngy, gr.at[2])
    near_rows = thirds(nb[...].reshape(128, 128))
    payload = payload_c + pick_rows(w_near, near_rows)
    m3s[...] = payload.reshape(ngx, 8, 128)
    spread(lambda k: m3s.at[gxd(k)[0]], m3r, i, ngx, gxd, gs.at[3], gr.at[3])
    m3r[i] = m3s[i]
    top_src = top_bound * pick_rows(w_top, near_rows)
    for _ in range(SWEEPS):
        top_t = sweep(top_t, top_up, top_dn, top_lf, top_rt, top_src, top_inv)
    m5s[...] = pick_rows(w_back, thirds(top_t)).reshape(ngy, 8, 128)
    spread(lambda k: m5s.at[gyd(k)[1]], m5r, j, ngy, gyd, gs.at[5], gr.at[5])
    m5r[j] = m5s[j]

    layers, width = st_ref.shape[1:]
    lines = 2 * layers
    temps = st_ref[...].reshape(lines, width)
    srow = lax.rem(iota((lines, width), 0), layers)
    c_up, c_dn, c_lf, c_rt = conductances(sc_ref[...].reshape(lines, width), layers)
    cool = cool_ref[...]

    def per_block(a, b):
        return jnp.concatenate(
            [jnp.broadcast_to(a, (layers, width)), jnp.broadcast_to(b, (layers, width))], axis=0
        )

    cool_at = per_block(cool[0:1], cool[1:2])

    y1[1]()
    x1[1]()

    def second_body(x, carry):
        t1p[x + 1, PAD - 1 : PAD, :] = y1_recv[0, x]
        t1p[x + 1, PAD + ny : PAD + ny + 1, :] = y1_recv[1, x]
        for yt in range(0, ny, 8):
            fluid_ref[x, pl.ds(yt, 8)] = stencil(t1p, x, yt, lambda n: coef[n, x, pl.ds(yt, 8)])
        return carry

    lax.fori_loop(0, nx, second_body, 0, unroll=4)

    all_in(m3r, ngx, gr.at[3])
    arrived = m3r[0]
    for k in range(1, ngx):
        arrived = arrived + m3r[k]
    heat = WALL_RATIO * arrived[2:4]
    flux = heat * arrived[0:2]
    is_wall, is_cool = srow == 0, srow == layers - 1
    bound = jnp.where(is_wall, per_block(heat[0:1], heat[1:2]), jnp.where(is_cool, COOL, 0.0))
    source = jnp.where(is_wall, per_block(flux[0:1], flux[1:2]), jnp.where(is_cool, COOL * cool_at, 0.0))
    inverse = 1.0 / (c_up + c_dn + c_lf + c_rt + bound)
    for _ in range(SWEEPS):
        temps = sweep(temps, c_up, c_dn, c_lf, c_rt, source, inverse)
    solid_ref[...] = temps.reshape(2, layers, width)

    for group in (wy, wx, ys, xt, xk, xu, y1, x1):
        group[2]()
    for copy, sends, gets in corners:
        pl.when(sends)(copy.wait_send)
    all_in(cbuf, ngx, gs.at[0])
    all_in(cc, ngy, gs.at[1])
    all_in(nb, ngy, gs.at[2])
    all_in(m3r, ngx, gs.at[3])
    all_in(tops, ngx, gs.at[4])
    all_in(m5r, ngy, gs.at[5])

    all_in(m5r, ngy, gr.at[5])
    back = m5r[0]
    for k in range(1, ngy):
        back = back + m5r[k]
    per = 128 // ny
    lines_out = []
    shifted = [back if s == 0 else pltpu.roll(back, 128 - s * ny, 1) for s in range(per)]
    for x in range(nx):
        lines_out.append(shifted[x % per][x // per : x // per + 1, 0:ny])
    full = jnp.concatenate(lines_out, axis=0)
    is_live = iota((nx, ny), 0) // per < count_ref[0]
    wallout_ref[...] = jnp.where(is_live, full, wall_ref[...])


def finish(fluid, wall, solid, fluid_ref, wall_ref, solid_ref, sem):
    copies = [
        pltpu.make_async_copy(src, dst, sem.at[n])
        for n, (src, dst) in enumerate(((fluid, fluid_ref), (wall, wall_ref), (solid, solid_ref)))
    ]
    for copy in copies:
        copy.start()
    for copy in copies:
        copy.wait()


def solution(mesh):
    ngx, ngy = mesh.shape["gx"], mesh.shape["gy"]

    def shards(temp, kappa, vel, wall, count, fmap, stemp, scond, cool):
        nx, ny, nz = temp.shape
        cells, ndev = nx * ny, ngx * ngy
        vmem = pl.BlockSpec(memory_space=pltpu.VMEM)
        hbm = pl.BlockSpec(memory_space=pl.ANY)
        padded = (nx + 2, ny + 2 * PAD, nz)
        dma = pltpu.SemaphoreType.DMA
        out = pl.pallas_call(
            functools.partial(kernel, ngx, ngy),
            out_shape=(
                pltpu.VMEM(temp.shape, F32),
                pltpu.VMEM(wall.shape, F32),
                pltpu.VMEM(stemp.shape, F32),
            ),
            in_specs=[hbm, hbm, hbm, vmem, pl.BlockSpec(memory_space=pltpu.SMEM), vmem, vmem, vmem, vmem],
            out_specs=(vmem, vmem, vmem),
            scratch_shapes=[
                pltpu.VMEM(padded, F32),
                pltpu.VMEM(padded, F32),
                pltpu.VMEM(padded, F32),
                pltpu.VMEM((nx + 2, ny, nz), F32),
                pltpu.VMEM((nx, ny + 2 * PAD, nz), F32),
                pltpu.VMEM((nx, ny, nz), F32),
                pltpu.VMEM((7, nx, ny, nz), F32),
                pltpu.VMEM((nx, ny, nz), jnp.bfloat16),
                pltpu.VMEM((3, nx, ny, nz), jnp.bfloat16),
                pltpu.VMEM((nx, ny, 128), F32),
                pltpu.VMEM((2, 3, nx, 1, nz), F32),
                pltpu.VMEM((2, 3, nx, 1, nz), F32),
                pltpu.VMEM((2, nx, 1, nz), F32),
                pltpu.VMEM((2, nx, 1, nz), F32),
                pltpu.VMEM((8, cells), F32),
                pltpu.VMEM((2, 8, cells), F32),
                pltpu.VMEM((2, 8, 128), F32),
                pltpu.VMEM((2, 8, 128), F32),
                pltpu.VMEM((2, 2, 8, 128), F32),
                pltpu.VMEM((ngx, 8, 128), F32),
                pltpu.VMEM((8, 128), F32),
                pltpu.VMEM((ngy, 16, 128), F32),
                pltpu.VMEM((ngy, 8, 128), F32),
                pltpu.VMEM((ngx, 8, 128), F32),
                pltpu.VMEM((ngx, 8, 128), F32),
                pltpu.VMEM((ngx, 32, 128), F32),
                pltpu.VMEM((ngy, 8, 128), F32),
                pltpu.VMEM((ngy, 8, 128), F32),
                dma((3, 2)),
                dma((4, 2)),
                dma((4, 2)),
                dma((2, 2)),
                dma((2, 2)),
                dma((2, 2)),
                dma((2, 2)),
                dma((2, 2)),
                dma((2, 2)),
                dma((6,)),
                dma((6,)),
            ],
            compiler_params=pltpu.CompilerParams(
                collective_id=0, has_side_effects=True, vmem_limit_bytes=60 << 20
            ),
            name="coupled_step",
        )(temp, kappa, vel, wall, count, fmap.reshape(1, -1), stemp, scond, cool)
        return pl.pallas_call(
            finish,
            out_shape=(
                jax.ShapeDtypeStruct(temp.shape, F32),
                jax.ShapeDtypeStruct(wall.shape, F32),
                jax.ShapeDtypeStruct(stemp.shape, F32),
            ),
            in_specs=[vmem] * 3,
            out_specs=(hbm,) * 3,
            scratch_shapes=[dma((3,))],
            compiler_params=pltpu.CompilerParams(vmem_limit_bytes=1 << 20),
            name="write_out",
        )(*[pltpu.with_memory_space_constraint(o, pltpu.VMEM) for o in out])

    return jax.shard_map(
        shards,
        mesh=mesh,
        in_specs=(
            P("gx", "gy", None),
            P("gx", "gy", None),
            P(None, "gx", "gy", None),
            P("gx", "gy"),
            P(("gx", "gy")),
            P(),
            P(("gx", "gy"), None, None),
            P(("gx", "gy"), None, None),
            P(("gx", "gy"), None),
        ),
        out_specs=(P("gx", "gy", None), P("gx", "gy"), P(("gx", "gy"), None, None)),
        check_vma=False,
    )
```

```python
import functools

import jax
import jax.numpy as jnp
from jax import lax
from jax.experimental import pallas as pl
from jax.experimental.pallas import tpu as pltpu
from jax.sharding import PartitionSpec as P

MESH = pl.DeviceIdType.MESH
F32 = jnp.float32
SWEEPS = 6
WALL_RATIO = 25.0
COOL = 1.0
EXACT = lax.Precision.HIGHEST
PAD = 8


def nt_dot(a, b, precision=None):
    return lax.dot_general(
        a, b, (((1,), (1,)), ((), ())), precision=precision, preferred_element_type=F32
    )


def iota(shape, axis):
    return lax.broadcasted_iota(jnp.int32, shape, axis)


def thirds(value):
    pieces = []
    for _ in range(3):
        piece = value.astype(jnp.bfloat16)
        pieces.append(piece)
        value = value - piece.astype(F32)
    return pieces


def thrice(onehot):
    return jnp.concatenate([onehot.astype(F32).astype(jnp.bfloat16)] * 3, axis=1)


def pick_rows(onehot3, value):
    return jnp.dot(onehot3, jnp.concatenate(thirds(value), axis=0), preferred_element_type=F32)


def across(temp, k0, own, n, kn, un, sign):
    return (k0 + kn) * (n - temp) - sign * (own + un) * (temp + n)


def upright(temp, k0, uz, wall):
    rows = temp.shape[0]
    first = iota(temp.shape, 0) == 0

    def above(value):
        return pltpu.roll(value, rows - 1, 0)

    def below(value, ground):
        return jnp.where(first, ground, pltpu.roll(value, 1, 0))

    out = temp + across(temp, k0, uz, above(temp), above(k0), above(uz), 1.0)
    return out + across(temp, k0, uz, below(temp, wall), below(k0, 0.0), below(uz, 0.0), -1.0)


def conductances(conds, layers):
    lines, width = conds.shape
    row, col = lax.rem(iota(conds.shape, 0), layers), iota(conds.shape, 1)
    up = jnp.where(row == 0, 0.0, 0.5 * (conds + pltpu.roll(conds, 1, 0)))
    down = jnp.where(row == layers - 1, 0.0, 0.5 * (conds + pltpu.roll(conds, lines - 1, 0)))
    left = jnp.where(col == 0, 0.0, 0.5 * (conds + pltpu.roll(conds, 1, 1)))
    right = jnp.where(col == width - 1, 0.0, 0.5 * (conds + pltpu.roll(conds, width - 1, 1)))
    return up, down, left, right


def sweep(temps, up, down, left, right, source, inverse):
    lines, width = temps.shape
    total = up * pltpu.roll(temps, 1, 0) + down * pltpu.roll(temps, lines - 1, 0)
    total = total + left * pltpu.roll(temps, 1, 1) + right * pltpu.roll(temps, width - 1, 1)
    return (total + source) * inverse


def kernel(
    ngx, ngy,
    t_hbm, k_hbm, v_hbm, wall_ref, count_ref, map_ref, st_ref, sc_ref, cool_ref,
    fluid_ref, wallout_ref, solid_ref,
    tp, t1p, kp, uxp, uyp, uzp, coef, kraw, vraw, wallb,
    ys_send, ys_recv, yh_send, yh_recv, y1_send, y1_recv,
    wy_send, wy_recv, wx_send, wx_recv, wd_recv,
    cbuf, csend, cc, nb, m3s, m3r, tops, m5s, m5r,
    ld_sem, hs, hr, t1s, t1r, ws, wr, wds, wdr, gs, gr,
):
    nx, ny, nz = t_hbm.shape
    cells = nx * ny
    nblk = cells // 128
    ndev = ngx * ngy
    nsolid = 2 * ndev
    i, j = lax.axis_index("gx"), lax.axis_index("gy")
    me = i * ngy + j

    def gxd(k):
        return (lax.rem(i + k + ngx, ngx), j)

    def gyd(k):
        return (i, lax.rem(j + k + ngy, ngy))

    barrier = pltpu.get_barrier_semaphore()
    peers = [gxd(k) for k in range(1, ngx)] + [gyd(k) for k in range(1, ngy)]
    peers += [(gxd(dx)[0], gyd(dy)[1]) for dx in (1, -1) for dy in (1, -1)]
    for peer in peers:
        pl.semaphore_signal(barrier, inc=1, device_id=peer, device_id_type=MESH)
    loads = []
    for part, zs in enumerate((pl.ds(0, 128), pl.ds(128, nz - 128))):
        inside = (pl.ds(1, nx), pl.ds(PAD, ny), zs)
        loads.append((
            pltpu.make_async_copy(t_hbm.at[:, :, zs], tp.at[inside], ld_sem.at[0, part]),
            pltpu.make_async_copy(k_hbm.at[:, :, zs], kraw.at[:, :, zs], ld_sem.at[1, part]),
            pltpu.make_async_copy(v_hbm.at[:, :, :, zs], vraw.at[:, :, :, zs], ld_sem.at[2, part]),
        ))
    for group in loads:
        for load in group:
            load.start()

    eye = iota((ny, ny), 0) == iota((ny, ny), 1)

    def wall_body(x, carry):
        line = wall_ref[pl.ds(x, 1), :]
        col = jnp.sum(jnp.where(eye, jnp.broadcast_to(line, (ny, ny)), 0.0), axis=1, keepdims=True)
        wallb[x] = jnp.broadcast_to(col, (ny, 128))
        return carry

    lax.fori_loop(0, nx, wall_body, 0)

    for cond, plane in ((i == 0, 0), (i == ngx - 1, nx + 1)):

        @pl.when(cond)
        def _():
            tp[plane] = jnp.zeros(tp.shape[1:], F32)
            t1p[plane] = jnp.zeros(t1p.shape[1:], F32)
            kp[plane] = jnp.zeros(kp.shape[1:], F32)
            uxp[plane] = jnp.zeros(uxp.shape[1:], F32)
            side = 0 if plane == 0 else 1
            wx_recv[side] = jnp.zeros(wx_recv.shape[1:], F32)
            wd_recv[side] = jnp.zeros(wd_recv.shape[1:], F32)

    for cond, side in ((j == 0, 0), (j == ngy - 1, 1)):

        @pl.when(cond)
        def _():
            ys_recv[side] = jnp.zeros(ys_recv.shape[1:], F32)
            yh_recv[side] = jnp.zeros(yh_recv.shape[1:], jnp.bfloat16)
            y1_recv[side] = jnp.zeros(y1_recv.shape[1:], F32)
            wy_recv[side] = jnp.zeros(wy_recv.shape[1:], F32)
            wd_recv[:, side] = jnp.zeros((2, 8, 128), F32)

    s_w = jnp.concatenate([wall_ref[x : x + 1, :] for x in range(nx)], axis=1)

    def halo(src_of, dst_of, send, recv, axis):
        def make(up):
            spot, size, dev = (i, ngx, gxd) if axis == 0 else (j, ngy, gyd)
            copy = pltpu.make_async_remote_copy(
                src_ref=src_of(up), dst_ref=dst_of(up),
                send_sem=send.at[up], recv_sem=recv.at[up],
                device_id=dev(1 if up else -1), device_id_type=MESH,
            )
            sends = spot < size - 1 if up else spot > 0
            gets = spot > 0 if up else spot < size - 1
            return copy, sends, gets

        pairs = [make(1), make(0)]

        def start():
            for copy, sends, gets in pairs:
                pl.when(sends)(copy.start)

        def wait_recv():
            for copy, sends, gets in pairs:
                pl.when(gets)(copy.wait_recv)

        def wait_send():
            for copy, sends, gets in pairs:
                pl.when(sends)(copy.wait_send)

        return start, wait_recv, wait_send

    wy = halo(lambda up: wy_send, lambda up: wy_recv.at[1 - up], ws.at[0], wr.at[0], 1)
    wx = halo(lambda up: wx_send.at[up], lambda up: wx_recv.at[1 - up], ws.at[1], wr.at[1], 0)
    corners = []
    for upx in (0, 1):
        for upy in (0, 1):
            copy = pltpu.make_async_remote_copy(
                src_ref=wx_send.at[upx], dst_ref=wd_recv.at[1 - upx, 1 - upy],
                send_sem=wds.at[upx, upy], recv_sem=wdr.at[upx, upy],
                device_id=(gxd(1 if upx else -1)[0], gyd(1 if upy else -1)[1]), device_id_type=MESH,
            )
            low_x, high_x, low_y, high_y = i > 0, i < ngx - 1, j > 0, j < ngy - 1
            sends = jnp.logical_and(high_x if upx else low_x, high_y if upy else low_y)
            gets = jnp.logical_and(low_x if upx else high_x, low_y if upy else high_y)
            corners.append((copy, sends, gets))
    ys = halo(lambda up: ys_send.at[up, 0], lambda up: ys_recv.at[1 - up, 0], hs.at[0], hr.at[0], 1)
    yh = halo(lambda up: yh_send.at[up], lambda up: yh_recv.at[1 - up], hs.at[4], hr.at[4], 1)

    def planes(ref, padded):
        rows = pl.ds(PAD, ny) if padded else pl.ds(0, ny)
        return (
            lambda up: ref.at[nx if up else 1, rows],
            lambda up: ref.at[0 if up else nx + 1, rows],
        )

    xt = halo(*planes(tp, True), hs.at[1], hr.at[1], 0)
    xk = halo(*planes(kp, True), hs.at[2], hr.at[2], 0)
    xu = halo(*planes(uxp, False), hs.at[3], hr.at[3], 0)
    y1 = halo(lambda up: y1_send.at[up], lambda up: y1_recv.at[1 - up], t1s.at[0], t1r.at[0], 1)
    x1 = halo(*planes(t1p, True), t1s.at[1], t1r.at[1], 0)

    for load in loads[0]:
        load.wait()

    counts = jnp.full((8, 128), count_ref[0], jnp.int32).astype(F32)
    csend[...] = counts
    tops[i, 0:16] = st_ref[:, 0:8].reshape(16, 128)
    tops[i, 16:32] = sc_ref[:, 0:8].reshape(16, 128)

    def spread(src, buf, slot, size, dev, sem, rsem):
        for k in range(1, size):
            pltpu.make_async_remote_copy(
                src_ref=src(k), dst_ref=buf.at[slot], send_sem=sem, recv_sem=rsem,
                device_id=dev(k), device_id_type=MESH,
            ).start()

    def all_in(buf, size, sem):
        part = buf.at[pl.ds(0, size - 1)]
        pltpu.make_async_copy(part, part, sem).wait()


    pick16 = (iota((8, 128), 0) == iota((8, 128), 1)).astype(F32).astype(jnp.bfloat16)

    def slab(value):
        return nt_dot(pick16, value.reshape(cells, 128))

    s_t = sum(nt_dot(pick16, piece) for piece in thirds(tp[1 : nx + 1, PAD : PAD + ny, 0:128].reshape(cells, 128)))
    s_k = 0.5 * slab(kraw[:, :, 0:128])
    s_ux = 0.25 * slab(vraw[0, :, :, 0:128])
    s_uy = 0.25 * slab(vraw[1, :, :, 0:128])
    s_uz = 0.25 * slab(vraw[2, :, :, 0:128])
    lane = iota((8, cells), 1)
    y_first, y_last = lax.rem(lane, ny) == 0, lax.rem(lane, ny) == ny - 1
    x_first, x_last = lane < ny, lane >= cells - ny
    partial = upright(s_t, s_k, s_uz, s_w)
    for shift, edge, own, sign in (
        (cells - ny, x_last, s_ux, 1.0), (ny, x_first, s_ux, -1.0),
        (cells - 1, y_last, s_uy, 1.0), (1, y_first, s_uy, -1.0),
    ):
        term = across(
            s_t, s_k, own, pltpu.roll(s_t, shift, 1), pltpu.roll(s_k, shift, 1), pltpu.roll(own, shift, 1), sign
        )
        partial = partial + jnp.where(edge, 0.0, term)
    wy_send[...] = jnp.concatenate([s_t[0:2], s_k[0:2], s_uy[0:2], partial[0:1], s_ux[0:1]], axis=0)
    for up, lanes in ((1, slice(cells - 128, cells)), (0, slice(0, 128))):
        wx_send[up] = jnp.concatenate(
            [s_t[0:2, lanes], s_k[0:2, lanes], s_ux[0:2, lanes], partial[0:1, lanes], s_uy[0:1, lanes]], axis=0
        )
    pl.semaphore_wait(barrier, len(peers))
    spread(lambda k: csend, cbuf, i, ngx, gxd, gs.at[0], gr.at[0])
    wy[0]()
    wx[0]()
    for copy, sends, gets in corners:
        pl.when(sends)(copy.start)
    for load in loads[1]:
        load.wait()

    def convert(x, carry):
        kv = 0.5 * kraw[x].astype(F32)
        kp[x + 1, PAD : PAD + ny, :] = kv
        uxp[x + 1] = 0.25 * vraw[0, x].astype(F32)
        uv = 0.25 * vraw[1, x].astype(F32)
        uyp[x, PAD : PAD + ny, :] = uv
        uzp[x] = 0.25 * vraw[2, x].astype(F32)
        ys_send[0, 0, x] = tp[x + 1, PAD : PAD + 1, :]
        ys_send[1, 0, x] = tp[x + 1, PAD + ny - 1 : PAD + ny, :]
        ys_send[0, 1, x] = kv[0:1]
        ys_send[1, 1, x] = kv[ny - 1 : ny]
        ys_send[0, 2, x] = uv[0:1]
        ys_send[1, 2, x] = uv[ny - 1 : ny]
        return carry

    lax.fori_loop(0, nx, convert, 0, unroll=4)
    for side in (0, 1):
        for part in (0, 1):
            yh_send[side, part] = ys_send[side, 1 + part, :, 0, :].astype(jnp.bfloat16)
    yh[0]()
    ys[0]()
    xk[0]()
    xu[0]()
    xt[0]()
    spread(lambda k: tops.at[i], tops, i, ngx, gxd, gs.at[4], gr.at[4])

    zlane = iota((8, nz), 1)
    z_first, z_last = zlane == 0, zlane == nz - 1

    def stencil(src, x, yt, co):
        y0 = PAD + yt
        mid = src[x + 1, y0 : y0 + 8, :]
        wall = jnp.concatenate([wallb[x, pl.ds(yt, 8)]] * (nz // 128), axis=1)
        down = jnp.where(z_first, wall, pltpu.roll(mid, 1, 1))
        out = co(0) * mid
        out = out + co(1) * src[x + 2, y0 : y0 + 8, :]
        out = out + co(2) * src[x, y0 : y0 + 8, :]
        out = out + co(3) * src[x + 1, y0 + 1 : y0 + 9, :]
        out = out + co(4) * src[x + 1, y0 - 1 : y0 + 7, :]
        out = out + co(5) * pltpu.roll(mid, nz - 1, 1)
        return out + co(6) * down

    def advance_first(x, yt):
        y0 = PAD + yt
        k0 = kp[x + 1, y0 : y0 + 8, :]
        ux0 = uxp[x + 1, yt : yt + 8, :]
        uy0 = uyp[x, y0 : y0 + 8, :]
        uz0 = uzp[x, yt : yt + 8, :]
        kk, uu = k0 + kp[x + 2, y0 : y0 + 8, :], ux0 + uxp[x + 2, yt : yt + 8, :]
        total, c1 = kk + uu, kk - uu
        kk, uu = k0 + kp[x, y0 : y0 + 8, :], ux0 + uxp[x, yt : yt + 8, :]
        total, c2 = total + (kk - uu), kk + uu
        kk, uu = k0 + kp[x + 1, y0 + 1 : y0 + 9, :], uy0 + uyp[x, y0 + 1 : y0 + 9, :]
        total, c3 = total + (kk + uu), kk - uu
        kk, uu = k0 + kp[x + 1, y0 - 1 : y0 + 7, :], uy0 + uyp[x, y0 - 1 : y0 + 7, :]
        total, c4 = total + (kk - uu), kk + uu
        low, high = k0 - uz0, k0 + uz0
        c5 = jnp.where(z_last, 0.0, low + pltpu.roll(low, nz - 1, 1))
        total = total + (high + jnp.where(z_last, 0.0, pltpu.roll(high, nz - 1, 1)))
        c6 = high + jnp.where(z_first, 0.0, pltpu.roll(high, 1, 1))
        total = total + (low + jnp.where(z_first, 0.0, pltpu.roll(low, 1, 1)))
        made = (1.0 - total, c1, c2, c3, c4, c5, c6)
        for n, value in enumerate(made):
            coef[n, x, pl.ds(yt, 8)] = value
        value = stencil(tp, x, yt, lambda n: made[n])
        t1p[x + 1, y0 : y0 + 8, :] = value
        return value

    middle = range(8, ny - 8, 8)

    def middle_body(x, carry):
        for yt in middle:
            advance_first(x, yt)
        return carry

    lax.fori_loop(1, nx - 1, middle_body, 0, unroll=5)

    cbuf[i] = counts
    cond_blocks = jnp.concatenate([s_k[0:1, 128 * b : 128 * b + 128] for b in range(nblk)], axis=0)
    all_in(cbuf, ngx, gr.at[0])
    row8 = iota((8, 128), 0)
    column = jnp.zeros((8, 128), F32)
    for k in range(ngx):
        column = column + jnp.where(row8 == k, cbuf[k], 0.0)
    cc[j, 0:8] = cond_blocks
    cc[j, 8:16] = column
    spread(lambda k: cc.at[j], cc, j, ngy, gyd, gs.at[1], gr.at[1])

    def widen(tile):
        return jnp.concatenate([tile] * (cells // 128), axis=1)

    def row_first(value, row):
        return pltpu.roll(value, 8 - row, 0) if row else value

    wy[1]()
    wx[1]()
    for copy, sends, gets in corners:
        pl.when(gets)(copy.wait_recv)
    diag = {
        (sx, sy): pltpu.roll(wd_recv[sx, sy], shift, 1)
        for sx, sy, shift in ((0, 0, 1), (1, 0, 128 - ny + 1 - ny), (0, 1, 2 * ny - 1), (1, 1, 127))
    }
    first = partial
    beside = []
    for edge, seen, own, shift, sign, along, side, there in (
        (x_last, widen(pltpu.roll(wx_recv[1], 128 - ny, 1)), s_ux, cells - ny, 1.0, "x", 1, i < ngx - 1),
        (x_first, widen(pltpu.roll(wx_recv[0], ny, 1)), s_ux, ny, -1.0, "x", 0, i > 0),
        (y_last, pltpu.roll(wy_recv[1], ny - 1, 1), s_uy, cells - 1, 1.0, "y", 1, j < ngy - 1),
        (y_first, pltpu.roll(wy_recv[0], cells - (ny - 1), 1), s_uy, 1, -1.0, "y", 0, j > 0),
    ):
        n, kn, un = seen, row_first(seen, 2), row_first(seen, 4)
        term = across(s_t, s_k, own, n, kn, un, sign)
        first = first + jnp.where(edge, term, 0.0)
        beyond = row_first(seen, 6) - term
        cross = row_first(seen, 7)
        for other in (0, 1):
            d = widen(diag[(side, other)] if along == "x" else diag[(other, side)])
            ends = (y_last if other else y_first) if along == "x" else (x_last if other else x_first)
            d_u = row_first(d, 7 if along == "x" else 4)
            corner = across(n, kn, cross, d, row_first(d, 2), d_u, 1.0 if other else -1.0)
            beyond = beyond + jnp.where(ends, corner, 0.0)
        beyond = beyond * there.astype(F32)
        k_side = jnp.where(edge, kn, pltpu.roll(s_k, shift, 1))
        u_side = jnp.where(edge, un, pltpu.roll(own, shift, 1))
        beside.append((edge, beyond, own, shift, sign, k_side, u_side))
    second = upright(first, s_k, s_uz, s_w)
    for edge, beyond, own, shift, sign, k_side, u_side in beside:
        n = jnp.where(edge, beyond, pltpu.roll(first, shift, 1))
        second = second + across(first, s_k, own, n, k_side, u_side, sign)
    nb[j] = jnp.concatenate([second[0:1, 128 * b : 128 * b + 128] for b in range(nblk)], axis=0)
    spread(lambda k: nb.at[j], nb, j, ngy, gyd, gs.at[2], gr.at[2])

    yh[1]()
    for side in (0, 1):
        for part in (0, 1):
            ys_recv[side, 1 + part, :, 0, :] = yh_recv[side, part].astype(F32)
    ys[1]()
    xk[1]()
    xu[1]()
    xt[1]()
    for x in (0, nx - 1):
        middle_body(x, 0)

    def edge_body(x, carry):
        for row, side in ((PAD - 1, 0), (PAD + ny, 1)):
            tp[x + 1, row : row + 1, :] = ys_recv[side, 0, x]
            kp[x + 1, row : row + 1, :] = ys_recv[side, 1, x]
            uyp[x, row : row + 1, :] = ys_recv[side, 2, x]
        y1_send[0, x] = advance_first(x, 0)[0:1]
        y1_send[1, x] = advance_first(x, ny - 8)[7:8]
        return carry

    lax.fori_loop(0, nx, edge_body, 0, unroll=4)
    y1[0]()
    x1[0]()

    all_in(cc, ngy, gr.at[1])
    q = iota((8, 128), 1)
    table = jnp.zeros((8, 128), F32)
    for k in range(ngy):
        table = table + jnp.where(q // nblk == k, cc[k, 8:16], 0.0)
    before = (iota((128, 128), 0) // nblk < iota((128, 128), 1) // nblk).astype(F32) * (1.0 / nblk)
    prefix = jnp.dot(table, before, precision=EXACT, preferred_element_type=F32)
    row_total = jnp.sum(table, axis=1, keepdims=True) * (1.0 / nblk)
    offset = jnp.sum(
        jnp.where(row8 == i, prefix, 0.0) + jnp.where(row8 < i, jnp.broadcast_to(row_total, (8, 128)), 0.0),
        axis=0, keepdims=True,
    )
    mine = jnp.sum(jnp.where(row8 == i, table, 0.0), axis=0, keepdims=True)
    slot = lax.rem(iota((1, 128), 1), nblk).astype(F32)
    live = slot < mine
    rank = jnp.where(live, offset + slot, -1.0)
    onehot = (iota((nsolid, 128), 0).astype(F32) == rank).astype(F32)
    fmap = map_ref[...].astype(F32)
    target = jnp.dot(fmap, onehot, precision=EXACT, preferred_element_type=F32)
    target = jnp.where(live, target, -1.0)
    line = iota((8 * ngx, 128), 0)
    kind = lax.rem(line, 8)
    owner = 2 * ((line // 8) * ngy + j)
    for_near = jnp.where(kind < 2, owner + kind, -2).astype(F32)
    for_cond = jnp.where((kind >= 2) & (kind < 4), owner + kind - 2, -2).astype(F32)
    top_line = iota((128, 128), 0)
    top_row = lax.rem(top_line, 8)
    top_block = top_line // 8
    top_id = jnp.where(top_row == 0, 2 * ((top_block // 2) * ngy + j) + lax.rem(top_block, 2), -2)
    w_top = (top_id.astype(F32) == target).astype(F32)
    w_back = thrice(jnp.transpose(w_top))
    w_near = jnp.concatenate([thrice(for_near == target), thrice(w_top)], axis=0)
    w_cond = jnp.concatenate([thrice(for_cond == target), thrice(w_top)], axis=0)
    picked = pick_rows(w_cond, cc[:, 0:8].reshape(128, 128))
    payload_c, top_cond = picked[: 8 * ngx], picked[8 * ngx :]
    all_in(tops, ngx, gr.at[4])
    top_t = tops[:, 0:16].reshape(128, 128)
    top_c = tops[:, 16:32].reshape(128, 128)
    top_up, top_dn, top_lf, top_rt = conductances(top_c, 8)
    top_bound = WALL_RATIO * top_cond
    top_inv = 1.0 / (top_up + top_dn + top_lf + top_rt + top_bound)

    all_in(nb, ngy, gr.at[2])
    picked = pick_rows(w_near, nb[...].reshape(128, 128))
    payload = payload_c + picked[: 8 * ngx]
    m3s[...] = payload.reshape(ngx, 8, 128)
    spread(lambda k: m3s.at[gxd(k)[0]], m3r, i, ngx, gxd, gs.at[3], gr.at[3])
    m3r[i] = m3s[i]
    top_src = top_bound * picked[8 * ngx :]
    for _ in range(SWEEPS):
        tiles = top_t.reshape(16, 8, 128)
        above, below = (pltpu.roll(tiles, n, 1).reshape(128, 128) for n in (1, 7))
        total = top_up * above + top_dn * below
        total = total + top_lf * pltpu.roll(top_t, 1, 1) + top_rt * pltpu.roll(top_t, 127, 1)
        top_t = (total + top_src) * top_inv
    m5s[...] = pick_rows(w_back, top_t).reshape(ngy, 8, 128)
    spread(lambda k: m5s.at[gyd(k)[1]], m5r, j, ngy, gyd, gs.at[5], gr.at[5])
    m5r[j] = m5s[j]

    layers, width = st_ref.shape[1:]
    lines = 2 * layers
    temps = st_ref[...].reshape(lines, width)
    srow = lax.rem(iota((lines, width), 0), layers)
    c_up, c_dn, c_lf, c_rt = conductances(sc_ref[...].reshape(lines, width), layers)
    cool = cool_ref[...]

    def per_block(a, b):
        return jnp.concatenate(
            [jnp.broadcast_to(a, (layers, width)), jnp.broadcast_to(b, (layers, width))], axis=0
        )

    cool_at = per_block(cool[0:1], cool[1:2])

    def advance_second(x, yt):
        fluid_ref[x, pl.ds(yt, 8)] = stencil(t1p, x, yt, lambda n: coef[n, x, pl.ds(yt, 8)])

    def second_middle(x, carry):
        for yt in middle:
            advance_second(x, yt)
        return carry

    lax.fori_loop(1, nx - 1, second_middle, 0, unroll=5)
    y1[1]()
    x1[1]()
    for x in (0, nx - 1):
        second_middle(x, 0)

    def second_edge(x, carry):
        t1p[x + 1, PAD - 1 : PAD, :] = y1_recv[0, x]
        t1p[x + 1, PAD + ny : PAD + ny + 1, :] = y1_recv[1, x]
        for yt in (0, ny - 8):
            advance_second(x, yt)
        return carry

    lax.fori_loop(0, nx, second_edge, 0, unroll=4)

    all_in(m3r, ngx, gr.at[3])
    arrived = m3r[0]
    for k in range(1, ngx):
        arrived = arrived + m3r[k]
    heat = WALL_RATIO * arrived[2:4]
    flux = heat * arrived[0:2]
    is_wall, is_cool = srow == 0, srow == layers - 1
    bound = jnp.where(is_wall, per_block(heat[0:1], heat[1:2]), jnp.where(is_cool, COOL, 0.0))
    source = jnp.where(is_wall, per_block(flux[0:1], flux[1:2]), jnp.where(is_cool, COOL * cool_at, 0.0))
    inverse = 1.0 / (c_up + c_dn + c_lf + c_rt + bound)
    for _ in range(SWEEPS):
        temps = sweep(temps, c_up, c_dn, c_lf, c_rt, source, inverse)
    solid_ref[...] = temps.reshape(2, layers, width)

    for group in (wy, wx, ys, yh, xt, xk, xu, y1, x1):
        group[2]()
    for copy, sends, gets in corners:
        pl.when(sends)(copy.wait_send)
    all_in(cbuf, ngx, gs.at[0])
    all_in(cc, ngy, gs.at[1])
    all_in(nb, ngy, gs.at[2])
    all_in(m3r, ngx, gs.at[3])
    all_in(tops, ngx, gs.at[4])
    all_in(m5r, ngy, gs.at[5])

    all_in(m5r, ngy, gr.at[5])
    back = m5r[0]
    for k in range(1, ngy):
        back = back + m5r[k]
    per = 128 // ny
    lines_out = []
    shifted = [back if s == 0 else pltpu.roll(back, 128 - s * ny, 1) for s in range(per)]
    for x in range(nx):
        lines_out.append(shifted[x % per][x // per : x // per + 1, 0:ny])
    full = jnp.concatenate(lines_out, axis=0)
    is_live = iota((nx, ny), 0) // per < count_ref[0]
    wallout_ref[...] = jnp.where(is_live, full, wall_ref[...])


def finish(fluid, wall, solid, fluid_ref, wall_ref, solid_ref, sem):
    copies = [
        pltpu.make_async_copy(src, dst, sem.at[n])
        for n, (src, dst) in enumerate(((fluid, fluid_ref), (wall, wall_ref), (solid, solid_ref)))
    ]
    for copy in copies:
        copy.start()
    for copy in copies:
        copy.wait()


def solution(mesh):
    ngx, ngy = mesh.shape["gx"], mesh.shape["gy"]

    def shards(temp, kappa, vel, wall, count, fmap, stemp, scond, cool):
        nx, ny, nz = temp.shape
        cells, ndev = nx * ny, ngx * ngy
        vmem = pl.BlockSpec(memory_space=pltpu.VMEM)
        hbm = pl.BlockSpec(memory_space=pl.ANY)
        padded = (nx + 2, ny + 2 * PAD, nz)
        dma = pltpu.SemaphoreType.DMA
        out = pl.pallas_call(
            functools.partial(kernel, ngx, ngy),
            out_shape=(
                pltpu.VMEM(temp.shape, F32),
                pltpu.VMEM(wall.shape, F32),
                pltpu.VMEM(stemp.shape, F32),
            ),
            in_specs=[hbm, hbm, hbm, vmem, pl.BlockSpec(memory_space=pltpu.SMEM), vmem, vmem, vmem, vmem],
            out_specs=(vmem, vmem, vmem),
            scratch_shapes=[
                pltpu.VMEM(padded, F32),
                pltpu.VMEM(padded, F32),
                pltpu.VMEM(padded, F32),
                pltpu.VMEM((nx + 2, ny, nz), F32),
                pltpu.VMEM((nx, ny + 2 * PAD, nz), F32),
                pltpu.VMEM((nx, ny, nz), F32),
                pltpu.VMEM((7, nx, ny, nz), F32),
                pltpu.VMEM((nx, ny, nz), jnp.bfloat16),
                pltpu.VMEM((3, nx, ny, nz), jnp.bfloat16),
                pltpu.VMEM((nx, ny, 128), F32),
                pltpu.VMEM((2, 3, nx, 1, nz), F32),
                pltpu.VMEM((2, 3, nx, 1, nz), F32),
                pltpu.VMEM((2, 2, nx, nz), jnp.bfloat16),
                pltpu.VMEM((2, 2, nx, nz), jnp.bfloat16),
                pltpu.VMEM((2, nx, 1, nz), F32),
                pltpu.VMEM((2, nx, 1, nz), F32),
                pltpu.VMEM((8, cells), F32),
                pltpu.VMEM((2, 8, cells), F32),
                pltpu.VMEM((2, 8, 128), F32),
                pltpu.VMEM((2, 8, 128), F32),
                pltpu.VMEM((2, 2, 8, 128), F32),
                pltpu.VMEM((ngx, 8, 128), F32),
                pltpu.VMEM((8, 128), F32),
                pltpu.VMEM((ngy, 16, 128), F32),
                pltpu.VMEM((ngy, 8, 128), F32),
                pltpu.VMEM((ngx, 8, 128), F32),
                pltpu.VMEM((ngx, 8, 128), F32),
                pltpu.VMEM((ngx, 32, 128), F32),
                pltpu.VMEM((ngy, 8, 128), F32),
                pltpu.VMEM((ngy, 8, 128), F32),
                dma((3, 2)),
                dma((5, 2)),
                dma((5, 2)),
                dma((2, 2)),
                dma((2, 2)),
                dma((2, 2)),
                dma((2, 2)),
                dma((2, 2)),
                dma((2, 2)),
                dma((6,)),
                dma((6,)),
            ],
            compiler_params=pltpu.CompilerParams(
                collective_id=0, has_side_effects=True, vmem_limit_bytes=60 << 20
            ),
            name="coupled_step",
        )(temp, kappa, vel, wall, count, fmap.reshape(1, -1), stemp, scond, cool)
        return pl.pallas_call(
            finish,
            out_shape=(
                jax.ShapeDtypeStruct(temp.shape, F32),
                jax.ShapeDtypeStruct(wall.shape, F32),
                jax.ShapeDtypeStruct(stemp.shape, F32),
            ),
            in_specs=[vmem] * 3,
            out_specs=(hbm,) * 3,
            scratch_shapes=[dma((3,))],
            compiler_params=pltpu.CompilerParams(vmem_limit_bytes=1 << 20),
            name="write_out",
        )(*[pltpu.with_memory_space_constraint(o, pltpu.VMEM) for o in out])

    return jax.shard_map(
        shards,
        mesh=mesh,
        in_specs=(
            P("gx", "gy", None),
            P("gx", "gy", None),
            P(None, "gx", "gy", None),
            P("gx", "gy"),
            P(("gx", "gy")),
            P(),
            P(("gx", "gy"), None, None),
            P(("gx", "gy"), None, None),
            P(("gx", "gy"), None),
        ),
        out_specs=(P("gx", "gy", None), P("gx", "gy"), P(("gx", "gy"), None, None)),
        check_vma=False,
    )
```
